32 devices in a mesh: dp: 8 (over z, core), shard: 4 (over y, x).
Axes of the slice: x: 2, y: 2, z: 4, core: 2. Of those that a mesh axis runs over, the one named last changes fastest.
Arguments:
- points: bfloat16 [8192, 1024], P(('dp', 'shard'))
- first_center: bfloat16 [1024], replicated, may hold values from -0.1875 to 0.1875
- counts: int32 [3, 8, 4], P(None, 'dp', 'shard'), may hold values from 0 to 64, as said below
- cand_index: int32 [3, 8, 4, 64], P(None, 'dp', 'shard'), may hold values from 0 to 255, as said below
Outputs:
- min_dist: float32 [8192], P(('dp', 'shard'))
- weights: float32 [8192], P(('dp', 'shard'))
- potentials: float32 [4], replicated
The draws below stay inside these ranges and needn't reach their ends.
Inputs may be any that keep to these rules, and one draw needn't show every extreme that they name: In each round the counts of the 4 devices of one dp index sum to 64, so a round has 512 candidates; in each round and dp index some device has exactly 64. `cand_index`: each device's list in a round holds distinct local row numbers; only its first counts entries are candidates.
All inputs are finite; a program needn't handle non-finite values.
Results may differ from the reference program's by a relative error of at most 0.0003.
Values may be sent and summed in bfloat16 or wider, within the bound.
A program may use at most 64 MiB of HBM per device.

```python
import jax
import jax.numpy as jnp
from jax import lax

D = 1024
ROWS_DEV = 256
CANDS = 512
ROUNDS = 3
GROUPS = 8
GROUP_SIZE = 4
CAP = 64
GROUP_CANDS = 64
ROWS = 8192
DEVICES = 32


cluster_count = 256


def draw_points(key, part):
    keys = jax.random.split(key, 4)
    means = jax.random.normal(keys[0], (cluster_count, D), jnp.float32) / jnp.sqrt(float(D))
    member = jax.random.randint(keys[1], (ROWS,), 0, cluster_count)
    base = jnp.take(means, member, axis=0)
    trend = jnp.sqrt(1.0 + 2.0 * jnp.arange(ROWS, dtype=jnp.float32) / ROWS)[:, None]
    noise = 0.5 * jax.random.normal(keys[2], (ROWS, D), jnp.float32) / jnp.sqrt(float(D))
    spread = jnp.exp(jax.random.uniform(keys[3], (ROWS, 1), jnp.float32) * jnp.log(3.2))
    values = spread * trend * (base + noise)
    return values.astype(jnp.bfloat16)


def group_counts(key):
    key_hot, key_slots = jax.random.split(key)
    hot = jax.random.randint(key_hot, (), 0, GROUP_SIZE)
    slot_total = (GROUP_SIZE - 1) * CAP
    order = jax.random.permutation(key_slots, slot_total)
    taken = (jnp.arange(slot_total) < GROUP_CANDS - CAP).astype(jnp.int32)
    owner = order // CAP
    others = jnp.sum((owner[:, None] == jnp.arange(GROUP_SIZE - 1)[None, :]).astype(jnp.int32) * taken[:, None], axis=0)
    device = jnp.arange(GROUP_SIZE)
    other_pos = jnp.clip(device - (device > hot).astype(jnp.int32), 0, GROUP_SIZE - 2)
    return jnp.where(device == hot, CAP, jnp.take(others, other_pos)).astype(jnp.int32)


def draw_counts(key, part):
    keys = jax.random.split(jax.random.fold_in(key, 11), ROUNDS * GROUPS)
    values = jax.vmap(group_counts)(keys)
    return values.reshape(ROUNDS, GROUPS, GROUP_SIZE).astype(jnp.int32)


def draw_cand_index(key, part):
    keys = jax.random.split(jax.random.fold_in(key, 23), ROUNDS * GROUPS * GROUP_SIZE)
    values = jax.vmap(lambda k: jax.random.permutation(k, ROWS_DEV)[:CAP])(keys)
    return values.reshape(ROUNDS, GROUPS, GROUP_SIZE, CAP).astype(jnp.int32)


def scatter_about(stream_key, dims, scale, bound, held_as=jnp.bfloat16):
    return jnp.clip(scale * jax.random.normal(stream_key, dims, jnp.float32), -bound, bound).astype(held_as)


def setup_inputs(seed: int = 0) -> dict:
    streams_of = jax.random.split(jax.random.key(seed), 5)
    return {
        "points": draw_points(jax.random.fold_in(streams_of[4], 71), 0),
        "first_center": scatter_about(streams_of[1], (D,), D ** -0.5, 0.1875),
        "counts": draw_counts(jax.random.fold_in(streams_of[4], 71), 0),
        "cand_index": draw_cand_index(jax.random.fold_in(streams_of[4], 71), 0),
    }


def pair_dist(rows, cands):
    prod = jnp.dot(rows, cands.T, preferred_element_type=jnp.float32)
    rows_norm = jnp.sum(jnp.square(rows.astype(jnp.float32)), axis=1)
    cand_norm = jnp.sum(jnp.square(cands.astype(jnp.float32)), axis=1)
    return jnp.maximum(rows_norm[:, None] + cand_norm[None, :] - 2.0 * prod, 0.0)


def block_min(points, cands):
    block_rows = ROWS_DEV * 8
    blocks = points.reshape(ROWS // block_rows, block_rows, D)
    least = lax.map(lambda blk: jnp.min(pair_dist(blk, cands), axis=1), blocks)
    return least.reshape(ROWS)


def reference(points, first_center, counts, cand_index):
    running = block_min(points, first_center[None, :])
    sums = [jnp.sum(running)]
    for step in range(ROUNDS):
        each_count = counts[step].reshape(DEVICES)
        local_rows = cand_index[step].reshape(DEVICES, CAP)
        global_rows = jnp.arange(DEVICES, dtype=jnp.int32)[:, None] * ROWS_DEV + local_rows
        valid = jnp.arange(CAP, dtype=jnp.int32)[None, :] < each_count[:, None]
        chosen = jnp.nonzero(valid.reshape(-1), size=CANDS)[0].astype(jnp.int32)
        rows = jnp.take(global_rows.reshape(-1), chosen)
        cands = jnp.take(points, rows, axis=0)
        running = jnp.minimum(running, block_min(points, cands))
        sums.append(jnp.sum(running))
    potentials = jnp.stack(sums)
    weights = running * (ROWS / potentials[-1])
    return running, weights, potentials
```

```python
import functools

import jax
import jax.numpy as jnp
from jax import lax
from jax.experimental import pallas as pl
from jax.experimental.pallas import tpu as pltpu
from jax.sharding import PartitionSpec as P

CANDS_ALL = 512
QUAD = 4
TILE_ROWS = 16
LANES = 128
MESH = pl.DeviceIdType.MESH
CONTRACT_LAST = (((1,), (1,)), ((), ()))
CONTRACT_FIRST = (((0,), (0,)), ((), ()))


def round_kernel(
    groups,
    width,
    pts_hbm,
    fc_ref,
    cnt_ref,
    idx_ref,
    run_ref,
    wgt_ref,
    pot_ref,
    pts,
    packed,
    parts,
    cand,
    least_out,
    least_in,
    plane_sums,
    dp_sums,
    local_sem,
    part_send,
    part_recv,
    plane_send,
    plane_recv,
    class_send,
    class_recv,
    core_send,
    core_recv,
    z_send,
    z_recv,
    fwd_send,
    fwd_recv,
    least_send,
    least_recv,
    psum_send,
    psum_recv,
    dsum_send,
    dsum_recv,
):
    rounds, total = idx_ref.shape
    rows, depth = pts_hbm.shape
    each = total // width
    classes = groups // QUAD
    chunks = z_send.shape[0]
    chunk = rows // chunks

    dp, me = lax.axis_index("dp"), lax.axis_index("shard")
    cls, mine = dp // QUAD, dp % QUAD
    zside, core = mine // 2, mine % 2
    partner = zside * 2 + (1 - core)
    across = (1 - zside) * 2 + core
    diagonal = (1 - zside) * 2 + (1 - core)

    def copy(src, dst, send, recv, to):
        made = pltpu.make_async_remote_copy(
            src_ref=src, dst_ref=dst, send_sem=send, recv_sem=recv, device_id=to, device_id_type=MESH
        )
        made.start()
        sent.append(made)

    def arrived(dst, send, recv):
        pltpu.make_async_remote_copy(
            src_ref=dst,
            dst_ref=dst,
            send_sem=send,
            recv_sem=recv,
            device_id=(dp, lax.rem(me + 1, width)),
            device_id_type=MESH,
        ).wait_recv()

    sent = []
    in_quad = lambda k: (cls * QUAD + k, me)
    in_plane = lambda off: (dp, lax.rem(me + off, width))
    in_dp = lambda off: (lax.rem(dp + off, groups), me)
    in_class = lambda off: (lax.rem(dp + off * QUAD, groups), me)

    load = pltpu.make_async_copy(pts_hbm, pts.at[mine], local_sem)
    load.start()
    barrier = pltpu.get_barrier_semaphore()
    for off in range(1, width):
        pl.semaphore_signal(barrier, inc=1, device_id=in_plane(off), device_id_type=MESH)
    for off in range(1, groups):
        pl.semaphore_signal(barrier, inc=1, device_id=in_dp(off), device_id_type=MESH)
    load.wait()

    def pick(t):
        spot = lax.broadcasted_iota(jnp.int32, (rows, total), 0)
        slot = lax.broadcasted_iota(jnp.int32, (rows, total), 1)
        hit = (spot == idx_ref[t : t + 1, :]) & (slot < cnt_ref[t : t + 1, :])
        chosen = lax.dot_general(
            jnp.where(hit, 1.0, 0.0).astype(pts.dtype),
            pts[mine],
            CONTRACT_FIRST,
            preferred_element_type=jnp.float32,
        )
        packed[t] = chosen.astype(packed.dtype).reshape(width, each, depth)

    def scatter(t):
        for off in range(1, width):
            copy(
                packed.at[t, lax.rem(me + off, width)],
                parts.at[t, me],
                part_send.at[t, off - 1],
                part_recv.at[t, off - 1],
                in_plane(off),
            )

    pick(0)
    pl.semaphore_wait(barrier, width - 1 + groups - 1)
    scatter(0)
    for j in range(chunks):
        span = pl.ds(j * chunk, chunk)
        copy(pts_hbm.at[span], pts.at[mine, span], z_send.at[j], z_recv.at[j], in_quad(across))
    for t in range(1, rounds):
        pick(t)
        scatter(t)
    copy(pts_hbm, pts.at[mine], core_send, core_recv, in_quad(partner))

    squares = jnp.square(pts[mine].astype(jnp.float32))
    lanes = squares[:, :LANES]
    for j in range(1, depth // LANES):
        lanes = lanes + squares[:, j * LANES : (j + 1) * LANES]
    rows_norm = jnp.sum(lanes.T, axis=0, keepdims=True)
    first = fc_ref[...]
    first_norm = jnp.sum(jnp.square(first.astype(jnp.float32)), axis=1, keepdims=True)
    first_prod = lax.dot_general(
        jnp.broadcast_to(first, (TILE_ROWS, depth)),
        pts[mine],
        CONTRACT_LAST,
        preferred_element_type=jnp.float32,
    )[:1]
    running = jnp.maximum(rows_norm + first_norm - 2.0 * first_prod, 0.0)

    def spread(t, c, at):
        for off in range(1, width):
            copy(
                cand.at[t, c, me],
                cand.at[t, c, me],
                plane_send.at[t, at, off - 1],
                plane_recv.at[t, at, off - 1],
                in_plane(off),
            )

    for t in range(rounds):
        held = packed[t, me].astype(jnp.float32)
        for off in range(1, width):
            source = lax.rem(me - off + width, width)
            arrived(parts.at[t, source], part_send.at[t, off - 1], part_recv.at[t, off - 1])
            held = held + parts[t, source].astype(jnp.float32)
        cand[t, cls, me] = held.astype(cand.dtype)
        for off in range(1, classes):
            copy(
                cand.at[t, cls, me],
                cand.at[t, cls, me],
                class_send.at[t, off - 1],
                class_recv.at[t, off - 1],
                in_class(off),
            )
        spread(t, cls, 0)
    for t in range(rounds):
        for off in range(1, classes):
            source = lax.rem(cls - off + classes, classes)
            arrived(cand.at[t, source, me], class_send.at[t, off - 1], class_recv.at[t, off - 1])
            spread(t, source, off)

    norms = []

    def centers(t):
        return cand[t].reshape(classes * width * each, depth)

    def least(t, k, lo, size):
        prod = lax.dot_general(
            centers(t), pts[k, lo : lo + size], CONTRACT_LAST, preferred_element_type=jnp.float32
        )
        least_out[k, t : t + 1, lo : lo + size] = jnp.min(
            norms[t] - 2.0 * prod, axis=0, keepdims=True
        )

    def give(k, at):
        copy(least_out.at[k], least_in.at[mine], least_send.at[at], least_recv.at[at], in_quad(k))

    least_out[...] = jnp.zeros_like(least_out)
    arrived(pts.at[partner], core_send, core_recv)
    for t in range(rounds):
        for at in range(classes):
            c = lax.rem(cls - at + classes, classes)
            for off in range(1, width):
                source = lax.rem(me - off + width, width)
                arrived(
                    cand.at[t, c, source],
                    plane_send.at[t, at, off - 1],
                    plane_recv.at[t, at, off - 1],
                )
        norms.append(
            jnp.sum(jnp.square(centers(t).astype(jnp.float32)), axis=1, keepdims=True)
        )
        least(t, mine, 0, rows)
        least(t, partner, 0, rows)
    give(partner, 0)
    for j in range(chunks):
        span = pl.ds(j * chunk, chunk)
        arrived(pts.at[across, span], z_send.at[j], z_recv.at[j])
        copy(
            pts.at[across, span], pts.at[across, span], fwd_send.at[j], fwd_recv.at[j], in_quad(partner)
        )
        for t in range(rounds):
            least(t, across, j * chunk, chunk)
    give(across, 1)
    for j in range(chunks):
        arrived(pts.at[diagonal, pl.ds(j * chunk, chunk)], fwd_send.at[j], fwd_recv.at[j])
        for t in range(rounds):
            least(t, diagonal, j * chunk, chunk)
    give(diagonal, 2)

    near = least_out[mine]
    for at, k in enumerate((partner, across, diagonal)):
        arrived(least_in.at[k], least_send.at[at], least_recv.at[at])
        near = jnp.minimum(near, least_in[k])

    def fold(row):
        out = row[:, :LANES]
        for j in range(1, rows // LANES):
            out = out + row[:, j * LANES : (j + 1) * LANES]
        return out

    partials = [fold(running)]
    for t in range(rounds):
        running = jnp.minimum(running, jnp.maximum(rows_norm + near[t : t + 1], 0.0))
        partials.append(fold(running))
    run_ref[...] = running

    tall = plane_sums.shape[1]
    partials += [jnp.zeros_like(partials[0])] * (tall - len(partials))
    plane_sums[me] = jnp.concatenate(partials, axis=0)
    for off in range(1, width):
        copy(
            plane_sums.at[me],
            plane_sums.at[me],
            psum_send.at[off - 1],
            psum_recv.at[off - 1],
            in_plane(off),
        )
    for off in range(1, width):
        source = lax.rem(me - off + width, width)
        arrived(plane_sums.at[source], psum_send.at[off - 1], psum_recv.at[off - 1])
    dp_sums[dp] = jnp.sum(plane_sums[...], axis=0)
    for off in range(1, groups):
        copy(
            dp_sums.at[dp], dp_sums.at[dp], dsum_send.at[off - 1], dsum_recv.at[off - 1], in_dp(off)
        )
    for off in range(1, groups):
        source = lax.rem(dp - off + groups, groups)
        arrived(dp_sums.at[source], dsum_send.at[off - 1], dsum_recv.at[off - 1])
    sums = jnp.sum(jnp.sum(dp_sums[...], axis=0), axis=1, keepdims=True)
    rows_all = rows * groups * width
    wgt_ref[...] = running * (rows_all / sums[rounds : rounds + 1])
    for t in range(rounds + 1):
        pot_ref[t] = sums[t, 0]
    for made in sent:
        made.wait_send()


def fused(points, first_center, counts, cand_index):
    rows, depth = points.shape
    rounds, total = counts.shape[0], cand_index.shape[3]
    groups, width = lax.axis_size("dp"), lax.axis_size("shard")
    each, classes = total // width, groups // QUAD
    chunks, tall = 2, 8
    f32, held = jnp.float32, points.dtype
    dma = pltpu.SemaphoreType.DMA
    vmem = pl.BlockSpec(memory_space=pltpu.VMEM)
    running, weights, potentials = pl.pallas_call(
        functools.partial(round_kernel, groups, width),
        out_shape=(
            jax.ShapeDtypeStruct((1, rows), f32),
            jax.ShapeDtypeStruct((1, rows), f32),
            jax.ShapeDtypeStruct((rounds + 1,), f32),
        ),
        in_specs=[pl.BlockSpec(memory_space=pl.ANY), vmem, vmem, vmem],
        out_specs=(vmem, vmem, pl.BlockSpec(memory_space=pltpu.SMEM)),
        scratch_shapes=[
            pltpu.VMEM((QUAD, rows, depth), held),
            pltpu.VMEM((rounds, width, each, depth), held),
            pltpu.VMEM((rounds, width, each, depth), held),
            pltpu.VMEM((rounds, classes, width, each, depth), held),
            pltpu.VMEM((QUAD, tall, rows), f32),
            pltpu.VMEM((QUAD, tall, rows), f32),
            pltpu.VMEM((width, tall, LANES), f32),
            pltpu.VMEM((groups, tall, LANES), f32),
            dma,
            dma((rounds, width - 1)),
            dma((rounds, width - 1)),
            dma((rounds, classes, width - 1)),
            dma((rounds, classes, width - 1)),
            dma((rounds, max(classes - 1, 1))),
            dma((rounds, max(classes - 1, 1))),
            dma,
            dma,
            dma((chunks,)),
            dma((chunks,)),
            dma((chunks,)),
            dma((chunks,)),
            dma((QUAD - 1,)),
            dma((QUAD - 1,)),
            dma((width - 1,)),
            dma((width - 1,)),
            dma((groups - 1,)),
            dma((groups - 1,)),
        ],
        compiler_params=pltpu.CompilerParams(
            collective_id=0, has_side_effects=True, vmem_limit_bytes=40 * 1024 * 1024
        ),
    )(
        points,
        first_center.reshape(1, depth),
        counts.reshape(rounds, 1),
        cand_index.reshape(rounds, total),
    )
    return running.reshape(rows), weights.reshape(rows), potentials


def one_holder(points, counts, cand_index):
    rows, depth = points.shape
    groups, width = lax.axis_size("dp"), lax.axis_size("shard")
    total = CANDS_ALL // groups
    return (
        cand_index.shape[3] == total
        and groups % QUAD == 0
        and width > 1
        and total % (width * TILE_ROWS) == 0
        and rows % (2 * LANES) == 0
        and depth % LANES == 0
        and counts.shape[0] < 8
    )


def pair_dist(rows, rows_norm, cands):
    prod = jnp.dot(rows, cands.T, preferred_element_type=jnp.float32)
    cand_norm = jnp.sum(jnp.square(cands.astype(jnp.float32)), axis=1)
    return jnp.maximum(rows_norm[:, None] + cand_norm[None, :] - 2.0 * prod, 0.0)


def pack_group(group_rows, member_counts, total, stride):
    ends = jnp.cumsum(member_counts)
    begins = ends - member_counts
    slot = jnp.arange(total, dtype=jnp.int32)
    source = jnp.sum((slot[:, None] >= ends[None, :]).astype(jnp.int32), axis=1)
    offset = slot - jnp.take(begins, source)
    return jnp.take(group_rows, source * stride + offset, axis=0)


def separate(points, first_center, counts, cand_index):
    rows_norm = jnp.sum(jnp.square(points.astype(jnp.float32)), axis=1)
    running = jnp.min(pair_dist(points, rows_norm, first_center[None, :]), axis=1)
    rounds = counts.shape[0]
    cap = cand_index.shape[3]
    every_count = lax.all_gather(counts.reshape(rounds, 1), ("dp", "shard"), axis=1, tiled=True)

    def global_sum(value):
        return lax.psum(value, ("dp", "shard"))

    partials = [jnp.sum(running)]
    totals = [global_sum(partials[0])]
    for step in range(rounds):
        local_rows = jnp.take(points, cand_index[step, 0, 0], axis=0)
        group_rows = lax.all_gather(local_rows, "shard", axis=0, tiled=True)
        width = lax.axis_size("shard")
        member_counts = lax.dynamic_slice_in_dim(
            every_count[step], lax.axis_index("dp") * width, width
        )
        total = CANDS_ALL // lax.axis_size("dp")
        packed = pack_group(group_rows, member_counts, total, cap)
        running = jnp.minimum(
            running,
            jnp.min(
                pair_dist(points, rows_norm, lax.all_gather(packed, "dp", axis=0, tiled=True)),
                axis=1,
            ),
        )
        partials.append(jnp.sum(running))
        totals.append(global_sum(partials[-1]))
    potentials = jnp.stack(totals)
    rows_total = points.shape[0] * lax.axis_size("dp") * lax.axis_size("shard")
    weights = running * (rows_total / potentials[-1])
    return (running, weights, potentials)


def body(points, first_center, counts, cand_index):
    if one_holder(points, counts, cand_index):
        return fused(points, first_center, counts, cand_index)
    return separate(points, first_center, counts, cand_index)


def solution(mesh):
    placed = (P(("dp", "shard"), None), P(), P(None, "dp", "shard"), P(None, "dp", "shard", None))
    return jax.shard_map(
        body,
        mesh=mesh,
        in_specs=placed,
        out_specs=(P(("dp", "shard")), P(("dp", "shard")), P()),
        check_vma=False,
    )
```

```python
import functools

import jax
import jax.numpy as jnp
from jax import lax
from jax.experimental import pallas as pl
from jax.experimental.pallas import tpu as pltpu
from jax.sharding import PartitionSpec as P

CANDS_ALL = 512
QUAD = 4
TILE_ROWS = 16
LANES = 128
MESH = pl.DeviceIdType.MESH
CONTRACT_LAST = (((1,), (1,)), ((), ()))
CONTRACT_FIRST = (((0,), (0,)), ((), ()))


def round_kernel(
    groups,
    width,
    pts_hbm,
    fc_hbm,
    cnt_hbm,
    idx_hbm,
    out_ref,
    fc_ref,
    cnt_ref,
    idx_ref,
    pts,
    packed,
    parts,
    cand,
    least_out,
    least_in,
    plane_sums,
    dp_sums,
    local_sems,
    part_send,
    part_recv,
    plane_send,
    plane_recv,
    class_send,
    class_recv,
    core_send,
    core_recv,
    z_send,
    z_recv,
    fwd_send,
    fwd_recv,
    least_send,
    least_recv,
    psum_send,
    psum_recv,
    dsum_send,
    dsum_recv,
):
    rounds, total = idx_ref.shape[0], idx_ref.shape[3]
    rows, depth = pts_hbm.shape
    each = total // width
    classes = groups // QUAD
    chunks = z_send.shape[0]
    chunk = rows // chunks

    dp, me = lax.axis_index("dp"), lax.axis_index("shard")
    cls, mine = dp // QUAD, dp % QUAD
    zside, core = mine // 2, mine % 2
    partner = zside * 2 + (1 - core)
    across = (1 - zside) * 2 + core
    diagonal = (1 - zside) * 2 + (1 - core)

    def copy(src, dst, send, recv, to):
        made = pltpu.make_async_remote_copy(
            src_ref=src, dst_ref=dst, send_sem=send, recv_sem=recv, device_id=to, device_id_type=MESH
        )
        made.start()
        sent.append(made)

    def arrived(dst, send, recv):
        pltpu.make_async_remote_copy(
            src_ref=dst,
            dst_ref=dst,
            send_sem=send,
            recv_sem=recv,
            device_id=(dp, lax.rem(me + 1, width)),
            device_id_type=MESH,
        ).wait_recv()

    sent = []
    in_quad = lambda k: (cls * QUAD + k, me)
    in_plane = lambda off: (dp, lax.rem(me + off, width))
    in_dp = lambda off: (lax.rem(dp + off, groups), me)
    in_class = lambda off: (lax.rem(dp + off * QUAD, groups), me)

    loads = [
        pltpu.make_async_copy(src, dst, local_sems.at[j])
        for j, (src, dst) in enumerate(
            (
                (idx_hbm, idx_ref),
                (cnt_hbm, cnt_ref),
                (pts_hbm, pts.at[mine]),
                (fc_hbm, fc_ref),
            )
        )
    ]
    for load in loads:
        load.start()
    barrier = pltpu.get_barrier_semaphore()
    for off in range(1, width):
        pl.semaphore_signal(barrier, inc=1, device_id=in_plane(off), device_id_type=MESH)
    for off in range(1, groups):
        pl.semaphore_signal(barrier, inc=1, device_id=in_dp(off), device_id_type=MESH)
    for load in loads:
        load.wait()

    def pick(t):
        spot = lax.broadcasted_iota(jnp.int32, (rows, total), 0)
        slot = lax.broadcasted_iota(jnp.int32, (rows, total), 1)
        hit = (spot == idx_ref[t, 0]) & (slot < cnt_ref[t])
        chosen = lax.dot_general(
            jnp.where(hit, 1.0, 0.0).astype(pts.dtype),
            pts[mine],
            CONTRACT_FIRST,
            preferred_element_type=jnp.float32,
        )
        packed[t] = chosen.astype(packed.dtype).reshape(width, each, depth)

    def scatter(t):
        for off in range(1, width):
            copy(
                packed.at[t, lax.rem(me + off, width)],
                parts.at[t, me],
                part_send.at[t, off - 1],
                part_recv.at[t, off - 1],
                in_plane(off),
            )

    pick(0)
    pl.semaphore_wait(barrier, width - 1 + groups - 1)
    scatter(0)

    def cross(j):
        span = pl.ds(j * chunk, chunk)
        copy(pts_hbm.at[span], pts.at[mine, span], z_send.at[j], z_recv.at[j], in_quad(across))

    cross(0)
    for t in range(1, rounds):
        pick(t)
        scatter(t)
    copy(pts_hbm, pts.at[mine], core_send, core_recv, in_quad(partner))

    squares = jnp.square(pts[mine].astype(jnp.float32))
    lanes = squares[:, :LANES]
    for j in range(1, depth // LANES):
        lanes = lanes + squares[:, j * LANES : (j + 1) * LANES]
    rows_norm = jnp.sum(lanes.T, axis=0, keepdims=True)
    first = fc_ref[...].reshape(1, depth)
    first_norm = jnp.sum(jnp.square(first.astype(jnp.float32)), axis=1, keepdims=True)
    first_prod = lax.dot_general(
        jnp.broadcast_to(first, (TILE_ROWS, depth)),
        pts[mine],
        CONTRACT_LAST,
        preferred_element_type=jnp.float32,
    )[:1]
    running = jnp.maximum(rows_norm + first_norm - 2.0 * first_prod, 0.0)

    def spread(t, c, at):
        for off in range(1, width):
            copy(
                cand.at[t, c, me],
                cand.at[t, c, me],
                plane_send.at[t, at, off - 1],
                plane_recv.at[t, at, off - 1],
                in_plane(off),
            )

    for t in range(rounds):
        held = packed[t, me].astype(jnp.float32)
        for off in range(1, width):
            source = lax.rem(me - off + width, width)
            arrived(parts.at[t, source], part_send.at[t, off - 1], part_recv.at[t, off - 1])
            held = held + parts[t, source].astype(jnp.float32)
        cand[t, cls, me] = held.astype(cand.dtype)
        for off in range(1, classes):
            copy(
                cand.at[t, cls, me],
                cand.at[t, cls, me],
                class_send.at[t, off - 1],
                class_recv.at[t, off - 1],
                in_class(off),
            )
        spread(t, cls, 0)
        for j in range(1 + t * (chunks - 1) // rounds, 1 + (t + 1) * (chunks - 1) // rounds):
            cross(j)
    for t in range(rounds):
        for off in range(1, classes):
            source = lax.rem(cls - off + classes, classes)
            arrived(cand.at[t, source, me], class_send.at[t, off - 1], class_recv.at[t, off - 1])
            spread(t, source, off)

    norms = []

    def centers(t):
        return cand[t].reshape(classes * width * each, depth)

    def least(t, k, lo, size):
        prod = lax.dot_general(
            centers(t), pts[k, lo : lo + size], CONTRACT_LAST, preferred_element_type=jnp.float32
        )
        least_out[k, t : t + 1, lo : lo + size] = jnp.min(
            norms[t] - 2.0 * prod, axis=0, keepdims=True
        )

    def give(k, at):
        copy(least_out.at[k], least_in.at[mine], least_send.at[at], least_recv.at[at], in_quad(k))

    least_out[...] = jnp.zeros_like(least_out)
    arrived(pts.at[partner], core_send, core_recv)
    for t in range(rounds):
        for at in range(classes):
            c = lax.rem(cls - at + classes, classes)
            for off in range(1, width):
                source = lax.rem(me - off + width, width)
                arrived(
                    cand.at[t, c, source],
                    plane_send.at[t, at, off - 1],
                    plane_recv.at[t, at, off - 1],
                )
        norms.append(
            jnp.sum(jnp.square(centers(t).astype(jnp.float32)), axis=1, keepdims=True)
        )
        least(t, mine, 0, rows)
        least(t, partner, 0, rows)
    give(partner, 0)
    for lo in range(0, rows, LANES):
        for j in range(lo // chunk, (lo + LANES) // chunk):
            span = pl.ds(j * chunk, chunk)
            arrived(pts.at[across, span], z_send.at[j], z_recv.at[j])
            copy(
                pts.at[across, span],
                pts.at[across, span],
                fwd_send.at[j],
                fwd_recv.at[j],
                in_quad(partner),
            )
        for t in range(rounds):
            least(t, across, lo, LANES)
    give(across, 1)
    for lo in range(0, rows, LANES):
        for j in range(lo // chunk, (lo + LANES) // chunk):
            arrived(pts.at[diagonal, pl.ds(j * chunk, chunk)], fwd_send.at[j], fwd_recv.at[j])
        for t in range(rounds):
            least(t, diagonal, lo, LANES)
    give(diagonal, 2)

    near = least_out[mine]
    for at, k in enumerate((partner, across, diagonal)):
        arrived(least_in.at[k], least_send.at[at], least_recv.at[at])
        near = jnp.minimum(near, least_in[k])

    def fold(row):
        out = row[:, :LANES]
        for j in range(1, rows // LANES):
            out = out + row[:, j * LANES : (j + 1) * LANES]
        return out

    partials = [fold(running)]
    for t in range(rounds):
        running = jnp.minimum(running, jnp.maximum(rows_norm + near[t : t + 1], 0.0))
        partials.append(fold(running))
    out_ref[0:1] = running

    tall = plane_sums.shape[1]
    partials += [jnp.zeros_like(partials[0])] * (tall - len(partials))
    plane_sums[me] = jnp.concatenate(partials, axis=0)
    for off in range(1, width):
        copy(
            plane_sums.at[me],
            plane_sums.at[me],
            psum_send.at[off - 1],
            psum_recv.at[off - 1],
            in_plane(off),
        )
    for off in range(1, width):
        source = lax.rem(me - off + width, width)
        arrived(plane_sums.at[source], psum_send.at[off - 1], psum_recv.at[off - 1])
    dp_sums[dp] = jnp.sum(plane_sums[...], axis=0)
    for off in range(1, groups):
        copy(
            dp_sums.at[dp], dp_sums.at[dp], dsum_send.at[off - 1], dsum_recv.at[off - 1], in_dp(off)
        )
    for off in range(1, groups):
        source = lax.rem(dp - off + groups, groups)
        arrived(dp_sums.at[source], dsum_send.at[off - 1], dsum_recv.at[off - 1])
    sums = jnp.sum(jnp.sum(dp_sums[...], axis=0), axis=1, keepdims=True)
    rows_all = rows * groups * width
    out_ref[1:2] = running * (rows_all / sums[rounds : rounds + 1])
    spot = lax.broadcasted_iota(jnp.int32, (tall, rows), 1)
    slot = lax.broadcasted_iota(jnp.int32, (tall, rows), 0)
    out_ref[2:3] = jnp.sum(jnp.where(spot == slot, sums, 0.0), axis=0, keepdims=True)
    for made in sent:
        made.wait_send()


def fused(points, first_center, counts, cand_index):
    rows, depth = points.shape
    rounds, total = counts.shape[0], cand_index.shape[3]
    groups, width = lax.axis_size("dp"), lax.axis_size("shard")
    each, classes = total // width, groups // QUAD
    chunks, tall = 4, 8
    f32, held = jnp.float32, points.dtype
    dma = pltpu.SemaphoreType.DMA
    vmem = pl.BlockSpec(memory_space=pltpu.VMEM)
    hbm = pl.BlockSpec(memory_space=pltpu.HBM)
    out = pl.pallas_call(
        functools.partial(round_kernel, groups, width),
        out_shape=jax.ShapeDtypeStruct((3, rows), f32),
        in_specs=[hbm] * 4,
        out_specs=vmem,
        scratch_shapes=[
            pltpu.VMEM((depth,), held),
            pltpu.SMEM((rounds,), counts.dtype),
            pltpu.VMEM(cand_index.shape, cand_index.dtype),
            pltpu.VMEM((QUAD, rows, depth), held),
            pltpu.VMEM((rounds, width, each, depth), held),
            pltpu.VMEM((rounds, width, each, depth), held),
            pltpu.VMEM((rounds, classes, width, each, depth), held),
            pltpu.VMEM((QUAD, tall, rows), f32),
            pltpu.VMEM((QUAD, tall, rows), f32),
            pltpu.VMEM((width, tall, LANES), f32),
            pltpu.VMEM((groups, tall, LANES), f32),
            dma((4,)),
            dma((rounds, width - 1)),
            dma((rounds, width - 1)),
            dma((rounds, classes, width - 1)),
            dma((rounds, classes, width - 1)),
            dma((rounds, max(classes - 1, 1))),
            dma((rounds, max(classes - 1, 1))),
            dma,
            dma,
            dma((chunks,)),
            dma((chunks,)),
            dma((chunks,)),
            dma((chunks,)),
            dma((QUAD - 1,)),
            dma((QUAD - 1,)),
            dma((width - 1,)),
            dma((width - 1,)),
            dma((groups - 1,)),
            dma((groups - 1,)),
        ],
        compiler_params=pltpu.CompilerParams(
            collective_id=0, has_side_effects=True, vmem_limit_bytes=62 * 1024 * 1024
        ),
    )(
        points,
        first_center,
        counts.reshape(rounds),
        cand_index,
    )
    return out[0], out[1], out[2, : rounds + 1]


def one_holder(points, counts, cand_index):
    rows, depth = points.shape
    groups, width = lax.axis_size("dp"), lax.axis_size("shard")
    total = CANDS_ALL // groups
    return (
        cand_index.shape[3] == total
        and groups % QUAD == 0
        and width > 1
        and total % (width * TILE_ROWS) == 0
        and rows % (2 * LANES) == 0
        and depth % LANES == 0
        and counts.shape[0] < 8
    )


def pair_dist(rows, rows_norm, cands):
    prod = jnp.dot(rows, cands.T, preferred_element_type=jnp.float32)
    cand_norm = jnp.sum(jnp.square(cands.astype(jnp.float32)), axis=1)
    return jnp.maximum(rows_norm[:, None] + cand_norm[None, :] - 2.0 * prod, 0.0)


def pack_group(group_rows, member_counts, total, stride):
    ends = jnp.cumsum(member_counts)
    begins = ends - member_counts
    slot = jnp.arange(total, dtype=jnp.int32)
    source = jnp.sum((slot[:, None] >= ends[None, :]).astype(jnp.int32), axis=1)
    offset = slot - jnp.take(begins, source)
    return jnp.take(group_rows, source * stride + offset, axis=0)


def separate(points, first_center, counts, cand_index):
    rows_norm = jnp.sum(jnp.square(points.astype(jnp.float32)), axis=1)
    running = jnp.min(pair_dist(points, rows_norm, first_center[None, :]), axis=1)
    rounds = counts.shape[0]
    cap = cand_index.shape[3]
    every_count = lax.all_gather(counts.reshape(rounds, 1), ("dp", "shard"), axis=1, tiled=True)

    def global_sum(value):
        return lax.psum(value, ("dp", "shard"))

    partials = [jnp.sum(running)]
    totals = [global_sum(partials[0])]
    for step in range(rounds):
        local_rows = jnp.take(points, cand_index[step, 0, 0], axis=0)
        group_rows = lax.all_gather(local_rows, "shard", axis=0, tiled=True)
        width = lax.axis_size("shard")
        member_counts = lax.dynamic_slice_in_dim(
            every_count[step], lax.axis_index("dp") * width, width
        )
        total = CANDS_ALL // lax.axis_size("dp")
        packed = pack_group(group_rows, member_counts, total, cap)
        running = jnp.minimum(
            running,
            jnp.min(
                pair_dist(points, rows_norm, lax.all_gather(packed, "dp", axis=0, tiled=True)),
                axis=1,
            ),
        )
        partials.append(jnp.sum(running))
        totals.append(global_sum(partials[-1]))
    potentials = jnp.stack(totals)
    rows_total = points.shape[0] * lax.axis_size("dp") * lax.axis_size("shard")
    weights = running * (rows_total / potentials[-1])
    return (running, weights, potentials)


def body(points, first_center, counts, cand_index):
    if one_holder(points, counts, cand_index):
        return fused(points, first_center, counts, cand_index)
    return separate(points, first_center, counts, cand_index)


def solution(mesh):
    placed = (P(("dp", "shard"), None), P(), P(None, "dp", "shard"), P(None, "dp", "shard", None))
    return jax.shard_map(
        body,
        mesh=mesh,
        in_specs=placed,
        out_specs=(P(("dp", "shard")), P(("dp", "shard")), P()),
        check_vma=False,
    )
```

```python
import functools

import jax
import jax.numpy as jnp
from jax import lax
from jax.experimental import pallas as pl
from jax.experimental.pallas import tpu as pltpu
from jax.sharding import PartitionSpec as P

CANDS_ALL = 512
QUAD = 4
TILE_ROWS = 16
LANES = 128
MESH = pl.DeviceIdType.MESH
CONTRACT_LAST = (((1,), (1,)), ((), ()))
CONTRACT_FIRST = (((0,), (0,)), ((), ()))


def round_kernel(
    groups,
    width,
    pts_hbm,
    fc_hbm,
    cnt_hbm,
    idx_hbm,
    out_ref,
    fc_ref,
    cnt_ref,
    idx_ref,
    pts,
    packed,
    parts,
    cand,
    least_out,
    least_in,
    plane_sums,
    dp_sums,
    local_sems,
    part_send,
    part_recv,
    plane_send,
    plane_recv,
    class_send,
    class_recv,
    core_send,
    core_recv,
    z_send,
    z_recv,
    fwd_send,
    fwd_recv,
    least_send,
    least_recv,
    psum_send,
    psum_recv,
    dsum_send,
    dsum_recv,
):
    rounds, total = idx_ref.shape[0], idx_ref.shape[3]
    rows, depth = pts_hbm.shape
    each = total // width
    classes = groups // QUAD
    chunks = z_send.shape[0]
    chunk = rows // chunks

    dp, me = lax.axis_index("dp"), lax.axis_index("shard")
    cls, mine = dp // QUAD, dp % QUAD
    zside, core = mine // 2, mine % 2
    partner = zside * 2 + (1 - core)
    across = (1 - zside) * 2 + core
    diagonal = (1 - zside) * 2 + (1 - core)

    def copy(src, dst, send, recv, to):
        made = pltpu.make_async_remote_copy(
            src_ref=src, dst_ref=dst, send_sem=send, recv_sem=recv, device_id=to, device_id_type=MESH
        )
        made.start()
        sent.append(made)

    def arrived(dst, send, recv):
        pltpu.make_async_remote_copy(
            src_ref=dst,
            dst_ref=dst,
            send_sem=send,
            recv_sem=recv,
            device_id=(dp, lax.rem(me + 1, width)),
            device_id_type=MESH,
        ).wait_recv()

    sent = []
    in_quad = lambda k: (cls * QUAD + k, me)
    in_plane = lambda off: (dp, lax.rem(me + off, width))
    in_dp = lambda off: (lax.rem(dp + off, groups), me)
    in_class = lambda off: (lax.rem(dp + off * QUAD, groups), me)

    loads = [
        pltpu.make_async_copy(src, dst, local_sems.at[j])
        for j, (src, dst) in enumerate(
            (
                (idx_hbm, idx_ref),
                (cnt_hbm, cnt_ref),
                (pts_hbm, pts.at[mine]),
                (fc_hbm, fc_ref),
            )
        )
    ]
    for load in loads:
        load.start()
    barrier = pltpu.get_barrier_semaphore()
    for off in range(1, width):
        pl.semaphore_signal(barrier, inc=1, device_id=in_plane(off), device_id_type=MESH)
    for off in range(1, groups):
        pl.semaphore_signal(barrier, inc=1, device_id=in_dp(off), device_id_type=MESH)
    for load in loads:
        load.wait()

    def cross(j):
        span = pl.ds(j * chunk, chunk)
        copy(pts_hbm.at[span], pts.at[mine, span], z_send.at[j], z_recv.at[j], in_quad(across))

    spot = lax.broadcasted_iota(jnp.int32, (rows, total), 0)
    slot = lax.broadcasted_iota(jnp.int32, (rows, total), 1)
    for t in range(rounds):
        hit = (spot == idx_ref[t, 0]) & (slot < cnt_ref[t])
        chosen = lax.dot_general(
            jnp.where(hit, 1.0, 0.0).astype(pts.dtype),
            pts[mine],
            CONTRACT_FIRST,
            preferred_element_type=jnp.float32,
        )
        packed[:, t] = chosen.astype(packed.dtype).reshape(width, each, depth)
    pl.semaphore_wait(barrier, width - 1 + groups - 1)
    for off in range(1, width):
        copy(
            packed.at[lax.rem(me + off, width)],
            parts.at[me],
            part_send.at[off - 1],
            part_recv.at[off - 1],
            in_plane(off),
        )
    cross(0)
    copy(pts_hbm, pts.at[mine], core_send, core_recv, in_quad(partner))

    squares = jnp.square(pts[mine].astype(jnp.float32))
    lanes = squares[:, :LANES]
    for j in range(1, depth // LANES):
        lanes = lanes + squares[:, j * LANES : (j + 1) * LANES]
    rows_norm = jnp.sum(lanes.T, axis=0, keepdims=True)
    first = fc_ref[...].reshape(1, depth)
    first_norm = jnp.sum(jnp.square(first.astype(jnp.float32)), axis=1, keepdims=True)
    first_prod = lax.dot_general(
        jnp.broadcast_to(first, (TILE_ROWS, depth)),
        pts[mine],
        CONTRACT_LAST,
        preferred_element_type=jnp.float32,
    )[:1]
    running = jnp.maximum(rows_norm + first_norm - 2.0 * first_prod, 0.0)

    def spread(c, at):
        for off in range(1, width):
            copy(
                cand.at[c, me],
                cand.at[c, me],
                plane_send.at[at, off - 1],
                plane_recv.at[at, off - 1],
                in_plane(off),
            )

    held = packed[me].astype(jnp.float32)
    for off in range(1, width):
        source = lax.rem(me - off + width, width)
        arrived(parts.at[source], part_send.at[off - 1], part_recv.at[off - 1])
        held = held + parts[source].astype(jnp.float32)
    cand[cls, me] = held.astype(cand.dtype)
    for off in range(1, classes):
        copy(
            cand.at[cls, me],
            cand.at[cls, me],
            class_send.at[off - 1],
            class_recv.at[off - 1],
            in_class(off),
        )
    spread(cls, 0)
    for j in range(1, chunks):
        cross(j)
    for off in range(1, classes):
        source = lax.rem(cls - off + classes, classes)
        arrived(cand.at[source, me], class_send.at[off - 1], class_recv.at[off - 1])
        spread(source, off)

    def centers(c):
        return cand[c].reshape(width * rounds * each, depth)

    def center_norms(c):
        return jnp.sum(jnp.square(centers(c).astype(jnp.float32)), axis=1, keepdims=True)

    def least(c, norms, k, lo, size):
        prod = lax.dot_general(
            centers(c), pts[k, lo : lo + size], CONTRACT_LAST, preferred_element_type=jnp.float32
        )
        dist = (norms - 2.0 * prod).reshape(width, rounds, each, size)
        return jnp.min(jnp.min(dist, axis=0), axis=1)

    def keep(k, lo, found):
        least_out[k, 0:rounds, lo : lo + found.shape[1]] = found

    def give(k, at):
        copy(least_out.at[k], least_in.at[mine], least_send.at[at], least_recv.at[at], in_quad(k))

    least_out[...] = jnp.zeros_like(least_out)
    near_parts = {}
    norms = []
    turn = [lax.rem(cls - at + classes, classes) for at in range(classes)]
    for at, c in enumerate(turn):
        for off in range(1, width):
            source = lax.rem(me - off + width, width)
            arrived(cand.at[c, source], plane_send.at[at, off - 1], plane_recv.at[at, off - 1])
        norms.append(center_norms(c))
        if at == 0:
            arrived(pts.at[partner], core_send, core_recv)
        for k, name in ((mine, 0), (partner, 1)):
            found = least(c, norms[at], k, 0, rows)
            near_parts[name] = found if at == 0 else jnp.minimum(near_parts[name], found)
    keep(mine, 0, near_parts[0])
    keep(partner, 0, near_parts[1])
    give(partner, 0)

    def least_all(k, lo, size):
        found = least(turn[0], norms[0], k, lo, size)
        for at in range(1, classes):
            found = jnp.minimum(found, least(turn[at], norms[at], k, lo, size))
        keep(k, lo, found)

    for j in range(chunks):
        span = pl.ds(j * chunk, chunk)
        arrived(pts.at[across, span], z_send.at[j], z_recv.at[j])
        copy(
            pts.at[across, span], pts.at[across, span], fwd_send.at[j], fwd_recv.at[j], in_quad(partner)
        )
    least_all(across, 0, rows)
    give(across, 1)
    for j in range(chunks):
        arrived(pts.at[diagonal, pl.ds(j * chunk, chunk)], fwd_send.at[j], fwd_recv.at[j])
    least_all(diagonal, 0, rows)
    give(diagonal, 2)

    near = least_out[mine]
    for at, k in enumerate((partner, across, diagonal)):
        arrived(least_in.at[k], least_send.at[at], least_recv.at[at])
        near = jnp.minimum(near, least_in[k])

    def fold(row):
        out = row[:, :LANES]
        for j in range(1, rows // LANES):
            out = out + row[:, j * LANES : (j + 1) * LANES]
        return out

    partials = [fold(running)]
    for t in range(rounds):
        running = jnp.minimum(running, jnp.maximum(rows_norm + near[t : t + 1], 0.0))
        partials.append(fold(running))
    out_ref[0:1] = running

    tall = plane_sums.shape[1]
    partials += [jnp.zeros_like(partials[0])] * (tall - len(partials))
    plane_sums[me] = jnp.concatenate(partials, axis=0)
    for off in range(1, width):
        copy(
            plane_sums.at[me],
            plane_sums.at[me],
            psum_send.at[off - 1],
            psum_recv.at[off - 1],
            in_plane(off),
        )
    for off in range(1, width):
        source = lax.rem(me - off + width, width)
        arrived(plane_sums.at[source], psum_send.at[off - 1], psum_recv.at[off - 1])
    dp_sums[dp] = jnp.sum(plane_sums[...], axis=0)
    for off in range(1, groups):
        copy(
            dp_sums.at[dp], dp_sums.at[dp], dsum_send.at[off - 1], dsum_recv.at[off - 1], in_dp(off)
        )
    for off in range(1, groups):
        source = lax.rem(dp - off + groups, groups)
        arrived(dp_sums.at[source], dsum_send.at[off - 1], dsum_recv.at[off - 1])
    sums = jnp.sum(jnp.sum(dp_sums[...], axis=0), axis=1, keepdims=True)
    rows_all = rows * groups * width
    out_ref[1:2] = running * (rows_all / sums[rounds : rounds + 1])
    spot = lax.broadcasted_iota(jnp.int32, (tall, rows), 1)
    slot = lax.broadcasted_iota(jnp.int32, (tall, rows), 0)
    out_ref[2:3] = jnp.sum(jnp.where(spot == slot, sums, 0.0), axis=0, keepdims=True)
    for made in sent:
        made.wait_send()


def fused(points, first_center, counts, cand_index):
    rows, depth = points.shape
    rounds, total = counts.shape[0], cand_index.shape[3]
    groups, width = lax.axis_size("dp"), lax.axis_size("shard")
    each, classes = total // width, groups // QUAD
    chunks, tall = 2, 8
    f32, held = jnp.float32, points.dtype
    dma = pltpu.SemaphoreType.DMA
    vmem = pl.BlockSpec(memory_space=pltpu.VMEM)
    hbm = pl.BlockSpec(memory_space=pltpu.HBM)
    out = pl.pallas_call(
        functools.partial(round_kernel, groups, width),
        out_shape=jax.ShapeDtypeStruct((3, rows), f32),
        in_specs=[hbm] * 4,
        out_specs=vmem,
        scratch_shapes=[
            pltpu.VMEM((depth,), held),
            pltpu.SMEM((rounds,), counts.dtype),
            pltpu.VMEM(cand_index.shape, cand_index.dtype),
            pltpu.VMEM((QUAD, rows, depth), held),
            pltpu.VMEM((width, rounds, each, depth), held),
            pltpu.VMEM((width, rounds, each, depth), held),
            pltpu.VMEM((classes, width, rounds, each, depth), held),
            pltpu.VMEM((QUAD, tall, rows), f32),
            pltpu.VMEM((QUAD, tall, rows), f32),
            pltpu.VMEM((width, tall, LANES), f32),
            pltpu.VMEM((groups, tall, LANES), f32),
            dma((4,)),
            dma((width - 1,)),
            dma((width - 1,)),
            dma((classes, width - 1)),
            dma((classes, width - 1)),
            dma((max(classes - 1, 1),)),
            dma((max(classes - 1, 1),)),
            dma,
            dma,
            dma((chunks,)),
            dma((chunks,)),
            dma((chunks,)),
            dma((chunks,)),
            dma((QUAD - 1,)),
            dma((QUAD - 1,)),
            dma((width - 1,)),
            dma((width - 1,)),
            dma((groups - 1,)),
            dma((groups - 1,)),
        ],
        compiler_params=pltpu.CompilerParams(
            collective_id=0, has_side_effects=True, vmem_limit_bytes=62 * 1024 * 1024
        ),
    )(
        points,
        first_center,
        counts.reshape(rounds),
        cand_index,
    )
    return out[0], out[1], out[2, : rounds + 1]


def one_holder(points, counts, cand_index):
    rows, depth = points.shape
    groups, width = lax.axis_size("dp"), lax.axis_size("shard")
    total = CANDS_ALL // groups
    return (
        cand_index.shape[3] == total
        and groups % QUAD == 0
        and width > 1
        and total % (width * TILE_ROWS) == 0
        and rows % (2 * LANES) == 0
        and depth % LANES == 0
        and counts.shape[0] < 8
    )


def pair_dist(rows, rows_norm, cands):
    prod = jnp.dot(rows, cands.T, preferred_element_type=jnp.float32)
    cand_norm = jnp.sum(jnp.square(cands.astype(jnp.float32)), axis=1)
    return jnp.maximum(rows_norm[:, None] + cand_norm[None, :] - 2.0 * prod, 0.0)


def pack_group(group_rows, member_counts, total, stride):
    ends = jnp.cumsum(member_counts)
    begins = ends - member_counts
    slot = jnp.arange(total, dtype=jnp.int32)
    source = jnp.sum((slot[:, None] >= ends[None, :]).astype(jnp.int32), axis=1)
    offset = slot - jnp.take(begins, source)
    return jnp.take(group_rows, source * stride + offset, axis=0)


def separate(points, first_center, counts, cand_index):
    rows_norm = jnp.sum(jnp.square(points.astype(jnp.float32)), axis=1)
    running = jnp.min(pair_dist(points, rows_norm, first_center[None, :]), axis=1)
    rounds = counts.shape[0]
    cap = cand_index.shape[3]
    every_count = lax.all_gather(counts.reshape(rounds, 1), ("dp", "shard"), axis=1, tiled=True)

    def global_sum(value):
        return lax.psum(value, ("dp", "shard"))

    partials = [jnp.sum(running)]
    totals = [global_sum(partials[0])]
    for step in range(rounds):
        local_rows = jnp.take(points, cand_index[step, 0, 0], axis=0)
        group_rows = lax.all_gather(local_rows, "shard", axis=0, tiled=True)
        width = lax.axis_size("shard")
        member_counts = lax.dynamic_slice_in_dim(
            every_count[step], lax.axis_index("dp") * width, width
        )
        total = CANDS_ALL // lax.axis_size("dp")
        packed = pack_group(group_rows, member_counts, total, cap)
        running = jnp.minimum(
            running,
            jnp.min(
                pair_dist(points, rows_norm, lax.all_gather(packed, "dp", axis=0, tiled=True)),
                axis=1,
            ),
        )
        partials.append(jnp.sum(running))
        totals.append(global_sum(partials[-1]))
    potentials = jnp.stack(totals)
    rows_total = points.shape[0] * lax.axis_size("dp") * lax.axis_size("shard")
    weights = running * (rows_total / potentials[-1])
    return (running, weights, potentials)


def body(points, first_center, counts, cand_index):
    if one_holder(points, counts, cand_index):
        return fused(points, first_center, counts, cand_index)
    return separate(points, first_center, counts, cand_index)


def solution(mesh):
    placed = (P(("dp", "shard"), None), P(), P(None, "dp", "shard"), P(None, "dp", "shard", None))
    return jax.shard_map(
        body,
        mesh=mesh,
        in_specs=placed,
        out_specs=(P(("dp", "shard")), P(("dp", "shard")), P()),
        check_vma=False,
    )
```

```python
import functools

import jax
import jax.numpy as jnp
from jax import lax
from jax.experimental import pallas as pl
from jax.experimental.pallas import tpu as pltpu
from jax.sharding import PartitionSpec as P

CANDS_ALL = 512
QUAD = 4
TILE_ROWS = 16
LANES = 128
MESH = pl.DeviceIdType.MESH
CONTRACT_LAST = (((1,), (1,)), ((), ()))
CONTRACT_FIRST = (((0,), (0,)), ((), ()))


def round_kernel(
    groups,
    width,
    pts_hbm,
    fc_hbm,
    cnt_hbm,
    idx_hbm,
    out_ref,
    fc_ref,
    cnt_ref,
    idx_ref,
    pts,
    packed,
    parts,
    cand,
    least_out,
    least_in,
    all_sums,
    local_sems,
    part_send,
    part_recv,
    plane_send,
    plane_recv,
    class_send,
    class_recv,
    core_send,
    core_recv,
    z_send,
    z_recv,
    fwd_send,
    fwd_recv,
    least_send,
    least_recv,
    sum_send,
    sum_recv,
):
    rounds, total = idx_ref.shape[0], idx_ref.shape[3]
    rows, depth = pts_hbm.shape
    each = total // width
    classes = groups // QUAD
    chunks = z_send.shape[0]
    chunk = rows // chunks

    dp, me = lax.axis_index("dp"), lax.axis_index("shard")
    cls, mine = dp // QUAD, dp % QUAD
    zside, core = mine // 2, mine % 2
    partner = zside * 2 + (1 - core)
    across = (1 - zside) * 2 + core
    diagonal = (1 - zside) * 2 + (1 - core)

    def copy(src, dst, send, recv, to):
        made = pltpu.make_async_remote_copy(
            src_ref=src, dst_ref=dst, send_sem=send, recv_sem=recv, device_id=to, device_id_type=MESH
        )
        made.start()
        sent.append(made)

    def arrived(dst, send, recv):
        pltpu.make_async_remote_copy(
            src_ref=dst,
            dst_ref=dst,
            send_sem=send,
            recv_sem=recv,
            device_id=(dp, lax.rem(me + 1, width)),
            device_id_type=MESH,
        ).wait_recv()

    sent = []
    in_quad = lambda k: (cls * QUAD + k, me)
    in_plane = lambda off: (dp, lax.rem(me + off, width))
    anyone = lambda a, b: (lax.rem(dp + a, groups), lax.rem(me + b, width))
    in_class = lambda off: (lax.rem(dp + off * QUAD, groups), me)

    loads = [
        pltpu.make_async_copy(src, dst, local_sems.at[j])
        for j, (src, dst) in enumerate(
            (
                (idx_hbm, idx_ref),
                (cnt_hbm, cnt_ref),
                (pts_hbm, pts.at[mine]),
                (fc_hbm, fc_ref),
            )
        )
    ]
    for load in loads:
        load.start()
    barrier = pltpu.get_barrier_semaphore()
    others = [(a, b) for a in range(groups) for b in range(width) if a or b]
    for a, b in others:
        pl.semaphore_signal(barrier, inc=1, device_id=anyone(a, b), device_id_type=MESH)
    for load in loads[:3]:
        load.wait()

    def cross(j):
        span = pl.ds(j * chunk, chunk)
        copy(pts_hbm.at[span], pts.at[mine, span], z_send.at[j], z_recv.at[j], in_quad(across))

    spot = lax.broadcasted_iota(jnp.int32, (rows, total), 0)
    slot = lax.broadcasted_iota(jnp.int32, (rows, total), 1)
    hits = [(spot == idx_ref[t, 0]) & (slot < cnt_ref[t]) for t in range(rounds)]
    chosen = lax.dot_general(
        jnp.concatenate([jnp.where(hit, 1.0, 0.0) for hit in hits], axis=1).astype(pts.dtype),
        pts[mine],
        CONTRACT_FIRST,
        preferred_element_type=jnp.float32,
    ).astype(packed.dtype)
    for t in range(rounds):
        packed[:, t] = chosen[t * total : (t + 1) * total].reshape(width, each, depth)
    pl.semaphore_wait(barrier, len(others))
    for off in range(1, width):
        copy(
            packed.at[lax.rem(me + off, width)],
            parts.at[me],
            part_send.at[off - 1],
            part_recv.at[off - 1],
            in_plane(off),
        )
    cross(0)
    copy(pts_hbm, pts.at[mine], core_send, core_recv, in_quad(partner))

    squares = jnp.square(pts[mine].astype(jnp.float32))
    lanes = squares[:, :LANES]
    for j in range(1, depth // LANES):
        lanes = lanes + squares[:, j * LANES : (j + 1) * LANES]
    rows_norm = jnp.sum(lanes.T, axis=0, keepdims=True)
    loads[3].wait()
    first = fc_ref[...].reshape(1, depth)
    first_norm = jnp.sum(jnp.square(first.astype(jnp.float32)), axis=1, keepdims=True)
    first_prod = lax.dot_general(
        jnp.broadcast_to(first, (TILE_ROWS, depth)),
        pts[mine],
        CONTRACT_LAST,
        preferred_element_type=jnp.float32,
    )[:1]
    running = jnp.maximum(rows_norm + first_norm - 2.0 * first_prod, 0.0)

    def spread(c, at):
        for off in range(1, width):
            copy(
                cand.at[c, me],
                cand.at[c, me],
                plane_send.at[at, off - 1],
                plane_recv.at[at, off - 1],
                in_plane(off),
            )

    held = packed[me].astype(jnp.float32)
    for off in range(1, width):
        source = lax.rem(me - off + width, width)
        arrived(parts.at[source], part_send.at[off - 1], part_recv.at[off - 1])
        held = held + parts[source].astype(jnp.float32)
    cand[cls, me] = held.astype(cand.dtype)
    for off in range(1, classes):
        copy(
            cand.at[cls, me],
            cand.at[cls, me],
            class_send.at[off - 1],
            class_recv.at[off - 1],
            in_class(off),
        )
    spread(cls, 0)
    for j in range(1, chunks):
        cross(j)
    for off in range(1, classes):
        source = lax.rem(cls - off + classes, classes)
        arrived(cand.at[source, me], class_send.at[off - 1], class_recv.at[off - 1])
        spread(source, off)

    def forward(j):
        span = pl.ds(j * chunk, chunk)
        arrived(pts.at[across, span], z_send.at[j], z_recv.at[j])
        copy(
            pts.at[across, span], pts.at[across, span], fwd_send.at[j], fwd_recv.at[j], in_quad(partner)
        )

    forward(0)

    def centers(c):
        return cand[c].reshape(width * rounds * each, depth)

    def center_norms(c):
        return jnp.sum(jnp.square(centers(c).astype(jnp.float32)), axis=1, keepdims=True)

    def least(c, norms, k, lo, size):
        prod = lax.dot_general(
            centers(c), pts[k, lo : lo + size], CONTRACT_LAST, preferred_element_type=jnp.float32
        )
        dist = (norms - 2.0 * prod).reshape(width, rounds, each, size)
        return jnp.min(jnp.min(dist, axis=0), axis=1)

    def keep(k, lo, found):
        least_out[k, 0:rounds, lo : lo + found.shape[1]] = found

    def give(k, at):
        copy(least_out.at[k], least_in.at[mine], least_send.at[at], least_recv.at[at], in_quad(k))

    least_out[...] = jnp.zeros_like(least_out)
    near_parts = {}
    norms = []
    turn = [lax.rem(cls - at + classes, classes) for at in range(classes)]
    for at, c in enumerate(turn):
        for off in range(1, width):
            source = lax.rem(me - off + width, width)
            arrived(cand.at[c, source], plane_send.at[at, off - 1], plane_recv.at[at, off - 1])
        norms.append(center_norms(c))
        if at == 0:
            arrived(pts.at[partner], core_send, core_recv)
        for k, name in ((mine, 0), (partner, 1)):
            found = least(c, norms[at], k, 0, rows)
            near_parts[name] = found if at == 0 else jnp.minimum(near_parts[name], found)
        if at == 0:
            for j in range(1, chunks):
                forward(j)
    keep(mine, 0, near_parts[0])
    keep(partner, 0, near_parts[1])
    give(partner, 0)

    def least_all(k, lo, size):
        found = least(turn[0], norms[0], k, lo, size)
        for at in range(1, classes):
            found = jnp.minimum(found, least(turn[at], norms[at], k, lo, size))
        keep(k, lo, found)

    least_all(across, 0, rows)
    give(across, 1)
    for j in range(chunks):
        arrived(pts.at[diagonal, pl.ds(j * chunk, chunk)], fwd_send.at[j], fwd_recv.at[j])
    least_all(diagonal, 0, rows)
    give(diagonal, 2)

    near = least_out[mine]
    for at, k in enumerate((partner, across, diagonal)):
        arrived(least_in.at[k], least_send.at[at], least_recv.at[at])
        near = jnp.minimum(near, least_in[k])

    def fold(row):
        out = row[:, :LANES]
        for j in range(1, rows // LANES):
            out = out + row[:, j * LANES : (j + 1) * LANES]
        return out

    partials = [fold(running)]
    for t in range(rounds):
        running = jnp.minimum(running, jnp.maximum(rows_norm + near[t : t + 1], 0.0))
        partials.append(fold(running))
    out_ref[0:1] = running

    tall = all_sums.shape[2]
    partials += [jnp.zeros_like(partials[0])] * (tall - len(partials))
    all_sums[dp, me] = jnp.concatenate(partials, axis=0)
    for a, b in others:
        copy(all_sums.at[dp, me], all_sums.at[dp, me], sum_send.at[a, b], sum_recv.at[a, b], anyone(a, b))
    for a, b in others:
        source = (lax.rem(dp - a + groups, groups), lax.rem(me - b + width, width))
        arrived(all_sums.at[source], sum_send.at[a, b], sum_recv.at[a, b])
    sums = jnp.sum(
        jnp.sum(all_sums[...].reshape(groups * width, tall, LANES), axis=0), axis=1, keepdims=True
    )
    rows_all = rows * groups * width
    out_ref[1:2] = running * (rows_all / sums[rounds : rounds + 1])
    spot = lax.broadcasted_iota(jnp.int32, (tall, rows), 1)
    slot = lax.broadcasted_iota(jnp.int32, (tall, rows), 0)
    out_ref[2:3] = jnp.sum(jnp.where(spot == slot, sums, 0.0), axis=0, keepdims=True)
    for made in sent:
        made.wait_send()


def fused(points, first_center, counts, cand_index):
    rows, depth = points.shape
    rounds, total = counts.shape[0], cand_index.shape[3]
    groups, width = lax.axis_size("dp"), lax.axis_size("shard")
    each, classes = total // width, groups // QUAD
    chunks, tall = 2, 8
    f32, held = jnp.float32, points.dtype
    dma = pltpu.SemaphoreType.DMA
    vmem = pl.BlockSpec(memory_space=pltpu.VMEM)
    hbm = pl.BlockSpec(memory_space=pltpu.HBM)
    out = pl.pallas_call(
        functools.partial(round_kernel, groups, width),
        out_shape=jax.ShapeDtypeStruct((3, rows), f32),
        in_specs=[hbm] * 4,
        out_specs=vmem,
        scratch_shapes=[
            pltpu.VMEM((depth,), held),
            pltpu.SMEM((rounds,), counts.dtype),
            pltpu.VMEM(cand_index.shape, cand_index.dtype),
            pltpu.VMEM((QUAD, rows, depth), held),
            pltpu.VMEM((width, rounds, each, depth), held),
            pltpu.VMEM((width, rounds, each, depth), held),
            pltpu.VMEM((classes, width, rounds, each, depth), held),
            pltpu.VMEM((QUAD, tall, rows), f32),
            pltpu.VMEM((QUAD, tall, rows), f32),
            pltpu.VMEM((groups, width, tall, LANES), f32),
            dma((4,)),
            dma((width - 1,)),
            dma((width - 1,)),
            dma((classes, width - 1)),
            dma((classes, width - 1)),
            dma((max(classes - 1, 1),)),
            dma((max(classes - 1, 1),)),
            dma,
            dma,
            dma((chunks,)),
            dma((chunks,)),
            dma((chunks,)),
            dma((chunks,)),
            dma((QUAD - 1,)),
            dma((QUAD - 1,)),
            dma((groups, width)),
            dma((groups, width)),
        ],
        compiler_params=pltpu.CompilerParams(
            collective_id=0, has_side_effects=True, vmem_limit_bytes=62 * 1024 * 1024
        ),
    )(
        points,
        first_center,
        counts.reshape(rounds),
        cand_index,
    )
    return out[0], out[1], out[2, : rounds + 1]


def one_holder(points, counts, cand_index):
    rows, depth = points.shape
    groups, width = lax.axis_size("dp"), lax.axis_size("shard")
    total = CANDS_ALL // groups
    return (
        cand_index.shape[3] == total
        and groups % QUAD == 0
        and width > 1
        and total % (width * TILE_ROWS) == 0
        and rows % (2 * LANES) == 0
        and depth % LANES == 0
        and counts.shape[0] < 8
    )


def pair_dist(rows, rows_norm, cands):
    prod = jnp.dot(rows, cands.T, preferred_element_type=jnp.float32)
    cand_norm = jnp.sum(jnp.square(cands.astype(jnp.float32)), axis=1)
    return jnp.maximum(rows_norm[:, None] + cand_norm[None, :] - 2.0 * prod, 0.0)


def pack_group(group_rows, member_counts, total, stride):
    ends = jnp.cumsum(member_counts)
    begins = ends - member_counts
    slot = jnp.arange(total, dtype=jnp.int32)
    source = jnp.sum((slot[:, None] >= ends[None, :]).astype(jnp.int32), axis=1)
    offset = slot - jnp.take(begins, source)
    return jnp.take(group_rows, source * stride + offset, axis=0)


def separate(points, first_center, counts, cand_index):
    rows_norm = jnp.sum(jnp.square(points.astype(jnp.float32)), axis=1)
    running = jnp.min(pair_dist(points, rows_norm, first_center[None, :]), axis=1)
    rounds = counts.shape[0]
    cap = cand_index.shape[3]
    every_count = lax.all_gather(counts.reshape(rounds, 1), ("dp", "shard"), axis=1, tiled=True)

    def global_sum(value):
        return lax.psum(value, ("dp", "shard"))

    partials = [jnp.sum(running)]
    totals = [global_sum(partials[0])]
    for step in range(rounds):
        local_rows = jnp.take(points, cand_index[step, 0, 0], axis=0)
        group_rows = lax.all_gather(local_rows, "shard", axis=0, tiled=True)
        width = lax.axis_size("shard")
        member_counts = lax.dynamic_slice_in_dim(
            every_count[step], lax.axis_index("dp") * width, width
        )
        total = CANDS_ALL // lax.axis_size("dp")
        packed = pack_group(group_rows, member_counts, total, cap)
        running = jnp.minimum(
            running,
            jnp.min(
                pair_dist(points, rows_norm, lax.all_gather(packed, "dp", axis=0, tiled=True)),
                axis=1,
            ),
        )
        partials.append(jnp.sum(running))
        totals.append(global_sum(partials[-1]))
    potentials = jnp.stack(totals)
    rows_total = points.shape[0] * lax.axis_size("dp") * lax.axis_size("shard")
    weights = running * (rows_total / potentials[-1])
    return (running, weights, potentials)


def body(points, first_center, counts, cand_index):
    if one_holder(points, counts, cand_index):
        return fused(points, first_center, counts, cand_index)
    return separate(points, first_center, counts, cand_index)


def solution(mesh):
    placed = (P(("dp", "shard"), None), P(), P(None, "dp", "shard"), P(None, "dp", "shard", None))
    return jax.shard_map(
        body,
        mesh=mesh,
        in_specs=placed,
        out_specs=(P(("dp", "shard")), P(("dp", "shard")), P()),
        check_vma=False,
    )
```

```python
import functools

import jax
import jax.numpy as jnp
from jax import lax
from jax.experimental import pallas as pl
from jax.experimental.pallas import tpu as pltpu
from jax.sharding import PartitionSpec as P

CANDS_ALL = 512
QUAD = 4
TILE_ROWS = 16
LANES = 128
VMEM_GRANT = 62 * 1024 * 1024
MESH = pl.DeviceIdType.MESH
CONTRACT_LAST = (((1,), (1,)), ((), ()))
CONTRACT_FIRST = (((0,), (0,)), ((), ()))


def round_kernel(
    groups,
    width,
    pts_hbm,
    fc_hbm,
    cnt_hbm,
    idx_hbm,
    run_ref,
    wgt_ref,
    pot_ref,
    fc_ref,
    cnt_ref,
    idx_ref,
    pts,
    packed,
    parts,
    cand,
    least_out,
    least_in,
    plane_sums,
    dp_sums,
    local_sems,
    part_send,
    part_recv,
    plane_send,
    plane_recv,
    class_send,
    class_recv,
    core_send,
    core_recv,
    z_send,
    z_recv,
    fwd_send,
    fwd_recv,
    least_send,
    least_recv,
    psum_send,
    psum_recv,
    dsum_send,
    dsum_recv,
):
    rounds, total = idx_ref.shape[0], idx_ref.shape[3]
    rows, depth = pts_hbm.shape
    each = total // width
    classes = groups // QUAD
    chunks = z_send.shape[0]
    chunk = rows // chunks

    dp, me = lax.axis_index("dp"), lax.axis_index("shard")
    cls, mine = dp // QUAD, dp % QUAD
    zside, core = mine // 2, mine % 2
    partner = zside * 2 + (1 - core)
    across = (1 - zside) * 2 + core
    diagonal = (1 - zside) * 2 + (1 - core)

    def copy(src, dst, send, recv, to):
        made = pltpu.make_async_remote_copy(
            src_ref=src, dst_ref=dst, send_sem=send, recv_sem=recv, device_id=to, device_id_type=MESH
        )
        made.start()
        sent.append(made)

    def arrived(dst, send, recv):
        pltpu.make_async_remote_copy(
            src_ref=dst,
            dst_ref=dst,
            send_sem=send,
            recv_sem=recv,
            device_id=(dp, lax.rem(me + 1, width)),
            device_id_type=MESH,
        ).wait_recv()

    sent = []
    in_quad = lambda k: (cls * QUAD + k, me)
    in_plane = lambda off: (dp, lax.rem(me + off, width))
    in_dp = lambda off: (lax.rem(dp + off, groups), me)
    in_class = lambda off: (lax.rem(dp + off * QUAD, groups), me)

    loads = [
        pltpu.make_async_copy(src, dst, local_sems.at[j])
        for j, (src, dst) in enumerate(
            (
                (idx_hbm, idx_ref),
                (cnt_hbm, cnt_ref),
                (pts_hbm, pts.at[mine]),
                (fc_hbm, fc_ref),
            )
        )
    ]
    for load in loads:
        load.start()
    barrier = pltpu.get_barrier_semaphore()
    for off in range(1, width):
        pl.semaphore_signal(barrier, inc=1, device_id=in_plane(off), device_id_type=MESH)
    for off in range(1, groups):
        pl.semaphore_signal(barrier, inc=1, device_id=in_dp(off), device_id_type=MESH)
    for load in loads[:3]:
        load.wait()

    def cross(j):
        span = pl.ds(j * chunk, chunk)
        copy(pts_hbm.at[span], pts.at[mine, span], z_send.at[j], z_recv.at[j], in_quad(across))

    spot = lax.broadcasted_iota(jnp.int32, (rows, total), 0)
    slot = lax.broadcasted_iota(jnp.int32, (rows, total), 1)
    hits = [(spot == idx_ref[t, 0]) & (slot < cnt_ref[t]) for t in range(rounds)]
    chosen = lax.dot_general(
        jnp.concatenate([jnp.where(hit, 1.0, 0.0) for hit in hits], axis=1).astype(pts.dtype),
        pts[mine],
        CONTRACT_FIRST,
        preferred_element_type=jnp.float32,
    ).astype(packed.dtype)
    for t in range(rounds):
        packed[:, t] = chosen[t * total : (t + 1) * total].reshape(width, each, depth)
    pl.semaphore_wait(barrier, width - 1 + groups - 1)
    for off in range(1, width):
        copy(
            packed.at[lax.rem(me + off, width)],
            parts.at[me],
            part_send.at[off - 1],
            part_recv.at[off - 1],
            in_plane(off),
        )
    cross(0)
    copy(pts_hbm, pts.at[mine], core_send, core_recv, in_quad(partner))

    squares = jnp.square(pts[mine].astype(jnp.float32))
    lanes = squares[:, :LANES]
    for j in range(1, depth // LANES):
        lanes = lanes + squares[:, j * LANES : (j + 1) * LANES]
    rows_norm = jnp.sum(lanes.T, axis=0, keepdims=True)
    loads[3].wait()
    first = fc_ref[...].reshape(1, depth)
    first_norm = jnp.sum(jnp.square(first.astype(jnp.float32)), axis=1, keepdims=True)
    first_prod = lax.dot_general(
        jnp.broadcast_to(first, (TILE_ROWS, depth)),
        pts[mine],
        CONTRACT_LAST,
        preferred_element_type=jnp.float32,
    )[:1]
    running = jnp.maximum(rows_norm + first_norm - 2.0 * first_prod, 0.0)

    def spread(c, at):
        for off in range(1, width):
            copy(
                cand.at[c, me],
                cand.at[c, me],
                plane_send.at[at, off - 1],
                plane_recv.at[at, off - 1],
                in_plane(off),
            )

    held = packed[me].astype(jnp.float32)
    for off in range(1, width):
        source = lax.rem(me - off + width, width)
        arrived(parts.at[source], part_send.at[off - 1], part_recv.at[off - 1])
        held = held + parts[source].astype(jnp.float32)
    cand[cls, me] = held.astype(cand.dtype)
    for off in range(1, classes):
        copy(
            cand.at[cls, me],
            cand.at[cls, me],
            class_send.at[off - 1],
            class_recv.at[off - 1],
            in_class(off),
        )
    spread(cls, 0)
    for j in range(1, chunks):
        cross(j)
    for off in range(1, classes):
        source = lax.rem(cls - off + classes, classes)
        arrived(cand.at[source, me], class_send.at[off - 1], class_recv.at[off - 1])
        spread(source, off)

    def forward(j):
        span = pl.ds(j * chunk, chunk)
        arrived(pts.at[across, span], z_send.at[j], z_recv.at[j])
        copy(
            pts.at[across, span], pts.at[across, span], fwd_send.at[j], fwd_recv.at[j], in_quad(partner)
        )

    forward(0)

    def centers(c):
        return cand[c].reshape(width * rounds * each, depth)

    def center_norms(c):
        return jnp.sum(jnp.square(centers(c).astype(jnp.float32)), axis=1, keepdims=True)

    def least(c, norms, k, lo, size):
        prod = lax.dot_general(
            centers(c), pts[k, lo : lo + size], CONTRACT_LAST, preferred_element_type=jnp.float32
        )
        dist = (norms - 2.0 * prod).reshape(width, rounds, each, size)
        return jnp.min(jnp.min(dist, axis=0), axis=1)

    def give(k, at):
        copy(least_out.at[k], least_in.at[mine], least_send.at[at], least_recv.at[at], in_quad(k))

    least_out[...] = jnp.zeros_like(least_out)
    turn = [lax.rem(cls - at + classes, classes) for at in range(classes)]
    found = {}
    for at, c in enumerate(turn):
        for off in range(1, width):
            source = lax.rem(me - off + width, width)
            arrived(cand.at[c, source], plane_send.at[at, off - 1], plane_recv.at[at, off - 1])
        norms = center_norms(c)
        for name, k in enumerate((mine, partner, across, diagonal)):
            if at == 0 and name == 1:
                arrived(pts.at[partner], core_send, core_recv)
            if at == 0 and name == 2:
                for j in range(1, chunks):
                    forward(j)
            if at == 0 and name == 3:
                for j in range(chunks):
                    span = pl.ds(j * chunk, chunk)
                    arrived(pts.at[diagonal, span], fwd_send.at[j], fwd_recv.at[j])
            this = least(c, norms, k, 0, rows)
            found[name] = this if at == 0 else jnp.minimum(found[name], this)
            if at == classes - 1:
                least_out[k, 0:rounds] = found[name]
                if name > 0:
                    give(k, name - 1)

    near = least_out[mine]
    for at, k in enumerate((partner, across, diagonal)):
        arrived(least_in.at[k], least_send.at[at], least_recv.at[at])
        near = jnp.minimum(near, least_in[k])

    def fold(row):
        out = row[:, :LANES]
        for j in range(1, rows // LANES):
            out = out + row[:, j * LANES : (j + 1) * LANES]
        return out

    partials = [fold(running)]
    for t in range(rounds):
        running = jnp.minimum(running, jnp.maximum(rows_norm + near[t : t + 1], 0.0))
        partials.append(fold(running))
    run_ref[...] = running

    tall = plane_sums.shape[1]
    partials += [jnp.zeros_like(partials[0])] * (tall - len(partials))
    plane_sums[me] = jnp.concatenate(partials, axis=0)
    for off in range(1, width):
        copy(
            plane_sums.at[me],
            plane_sums.at[me],
            psum_send.at[off - 1],
            psum_recv.at[off - 1],
            in_plane(off),
        )
    for off in range(1, width):
        source = lax.rem(me - off + width, width)
        arrived(plane_sums.at[source], psum_send.at[off - 1], psum_recv.at[off - 1])
    dp_sums[dp] = jnp.sum(plane_sums[...], axis=0)
    for off in range(1, groups):
        copy(
            dp_sums.at[dp], dp_sums.at[dp], dsum_send.at[off - 1], dsum_recv.at[off - 1], in_dp(off)
        )
    for off in range(1, groups):
        source = lax.rem(dp - off + groups, groups)
        arrived(dp_sums.at[source], dsum_send.at[off - 1], dsum_recv.at[off - 1])
    sums = jnp.sum(jnp.sum(dp_sums[...], axis=0), axis=1, keepdims=True)
    rows_all = rows * groups * width
    wgt_ref[...] = running * (rows_all / sums[rounds : rounds + 1])
    for t in range(rounds + 1):
        pot_ref[t] = sums[t, 0]
    for made in sent:
        made.wait_send()


def hand_on(*refs):
    *arrays, sems = refs
    count = len(arrays) // 2
    copies = [
        pltpu.make_async_copy(arrays[j], arrays[count + j], sems.at[j]) for j in range(count)
    ]
    for each in copies:
        each.start()
    for each in copies:
        each.wait()


def fused(points, first_center, counts, cand_index):
    rows, depth = points.shape
    rounds, total = counts.shape[0], cand_index.shape[3]
    groups, width = lax.axis_size("dp"), lax.axis_size("shard")
    each, classes = total // width, groups // QUAD
    chunks, tall = 2, 8
    f32, held = jnp.float32, points.dtype
    dma = pltpu.SemaphoreType.DMA
    vmem = pl.BlockSpec(memory_space=pltpu.VMEM)
    hbm = pl.BlockSpec(memory_space=pltpu.HBM)
    running, weights, potentials = pl.pallas_call(
        functools.partial(round_kernel, groups, width),
        out_shape=(
            jax.ShapeDtypeStruct((1, rows), f32),
            jax.ShapeDtypeStruct((1, rows), f32),
            jax.ShapeDtypeStruct((rounds + 1,), f32),
        ),
        in_specs=[hbm] * 4,
        out_specs=(vmem, vmem, pl.BlockSpec(memory_space=pltpu.SMEM)),
        scratch_shapes=[
            pltpu.VMEM((depth,), held),
            pltpu.SMEM((rounds,), counts.dtype),
            pltpu.VMEM(cand_index.shape, cand_index.dtype),
            pltpu.VMEM((QUAD, rows, depth), held),
            pltpu.VMEM((width, rounds, each, depth), held),
            pltpu.VMEM((width, rounds, each, depth), held),
            pltpu.VMEM((classes, width, rounds, each, depth), held),
            pltpu.VMEM((QUAD, tall, rows), f32),
            pltpu.VMEM((QUAD, tall, rows), f32),
            pltpu.VMEM((width, tall, LANES), f32),
            pltpu.VMEM((groups, tall, LANES), f32),
            dma((4,)),
            dma((width - 1,)),
            dma((width - 1,)),
            dma((classes, width - 1)),
            dma((classes, width - 1)),
            dma((max(classes - 1, 1),)),
            dma((max(classes - 1, 1),)),
            dma,
            dma,
            dma((chunks,)),
            dma((chunks,)),
            dma((chunks,)),
            dma((chunks,)),
            dma((QUAD - 1,)),
            dma((QUAD - 1,)),
            dma((width - 1,)),
            dma((width - 1,)),
            dma((groups - 1,)),
            dma((groups - 1,)),
        ],
        compiler_params=pltpu.CompilerParams(
            collective_id=0, has_side_effects=True, vmem_limit_bytes=VMEM_GRANT
        ),
    )(
        points,
        first_center,
        counts.reshape(rounds),
        cand_index,
    )
    made = (running.reshape(rows), weights.reshape(rows), potentials)
    return pl.pallas_call(
        hand_on,
        out_shape=[jax.ShapeDtypeStruct(part.shape, part.dtype) for part in made],
        in_specs=[hbm] * len(made),
        out_specs=[hbm] * len(made),
        scratch_shapes=[dma((len(made),))],
        compiler_params=pltpu.CompilerParams(vmem_limit_bytes=VMEM_GRANT),
    )(*made)


def one_holder(points, counts, cand_index):
    rows, depth = points.shape
    groups, width = lax.axis_size("dp"), lax.axis_size("shard")
    total = CANDS_ALL // groups
    return (
        cand_index.shape[3] == total
        and groups % QUAD == 0
        and width > 1
        and total % (width * TILE_ROWS) == 0
        and rows % (2 * LANES) == 0
        and depth % LANES == 0
        and counts.shape[0] < 8
    )


def pair_dist(rows, rows_norm, cands):
    prod = jnp.dot(rows, cands.T, preferred_element_type=jnp.float32)
    cand_norm = jnp.sum(jnp.square(cands.astype(jnp.float32)), axis=1)
    return jnp.maximum(rows_norm[:, None] + cand_norm[None, :] - 2.0 * prod, 0.0)


def pack_group(group_rows, member_counts, total, stride):
    ends = jnp.cumsum(member_counts)
    begins = ends - member_counts
    slot = jnp.arange(total, dtype=jnp.int32)
    source = jnp.sum((slot[:, None] >= ends[None, :]).astype(jnp.int32), axis=1)
    offset = slot - jnp.take(begins, source)
    return jnp.take(group_rows, source * stride + offset, axis=0)


def separate(points, first_center, counts, cand_index):
    rows_norm = jnp.sum(jnp.square(points.astype(jnp.float32)), axis=1)
    running = jnp.min(pair_dist(points, rows_norm, first_center[None, :]), axis=1)
    rounds = counts.shape[0]
    cap = cand_index.shape[3]
    every_count = lax.all_gather(counts.reshape(rounds, 1), ("dp", "shard"), axis=1, tiled=True)

    def global_sum(value):
        return lax.psum(value, ("dp", "shard"))

    partials = [jnp.sum(running)]
    totals = [global_sum(partials[0])]
    for step in range(rounds):
        local_rows = jnp.take(points, cand_index[step, 0, 0], axis=0)
        group_rows = lax.all_gather(local_rows, "shard", axis=0, tiled=True)
        width = lax.axis_size("shard")
        member_counts = lax.dynamic_slice_in_dim(
            every_count[step], lax.axis_index("dp") * width, width
        )
        total = CANDS_ALL // lax.axis_size("dp")
        packed = pack_group(group_rows, member_counts, total, cap)
        running = jnp.minimum(
            running,
            jnp.min(
                pair_dist(points, rows_norm, lax.all_gather(packed, "dp", axis=0, tiled=True)),
                axis=1,
            ),
        )
        partials.append(jnp.sum(running))
        totals.append(global_sum(partials[-1]))
    potentials = jnp.stack(totals)
    rows_total = points.shape[0] * lax.axis_size("dp") * lax.axis_size("shard")
    weights = running * (rows_total / potentials[-1])
    return (running, weights, potentials)


def body(points, first_center, counts, cand_index):
    if one_holder(points, counts, cand_index):
        return fused(points, first_center, counts, cand_index)
    return separate(points, first_center, counts, cand_index)


def solution(mesh):
    placed = (P(("dp", "shard"), None), P(), P(None, "dp", "shard"), P(None, "dp", "shard", None))
    return jax.shard_map(
        body,
        mesh=mesh,
        in_specs=placed,
        out_specs=(P(("dp", "shard")), P(("dp", "shard")), P()),
        check_vma=False,
    )
```

```python
import functools

import jax
import jax.numpy as jnp
from jax import lax
from jax.experimental import pallas as pl
from jax.experimental.pallas import tpu as pltpu
from jax.sharding import PartitionSpec as P

CANDS_ALL = 512
QUAD = 4
TILE_ROWS = 16
LANES = 128
VMEM_GRANT = 62 * 1024 * 1024
MESH = pl.DeviceIdType.MESH
CONTRACT_LAST = (((1,), (1,)), ((), ()))
CONTRACT_FIRST = (((0,), (0,)), ((), ()))


def round_kernel(
    groups,
    width,
    pts_hbm,
    fc_hbm,
    cnt_hbm,
    idx_hbm,
    run_ref,
    wgt_ref,
    pot_ref,
    fc_ref,
    cnt_ref,
    idx_ref,
    pts,
    packed,
    parts,
    cand,
    least_out,
    least_in,
    all_sums,
    local_sems,
    part_send,
    part_recv,
    plane_send,
    plane_recv,
    class_send,
    class_recv,
    core_send,
    core_recv,
    z_send,
    z_recv,
    fwd_send,
    fwd_recv,
    least_send,
    least_recv,
    sum_send,
    sum_recv,
):
    rounds, total = idx_ref.shape[0], idx_ref.shape[3]
    rows, depth = pts_hbm.shape
    each = total // width
    classes = groups // QUAD
    chunks = z_send.shape[0]
    chunk = rows // chunks

    dp, me = lax.axis_index("dp"), lax.axis_index("shard")
    cls, mine = dp // QUAD, dp % QUAD
    zside, core = mine // 2, mine % 2
    partner = zside * 2 + (1 - core)
    across = (1 - zside) * 2 + core
    diagonal = (1 - zside) * 2 + (1 - core)

    def copy(src, dst, send, recv, to):
        made = pltpu.make_async_remote_copy(
            src_ref=src, dst_ref=dst, send_sem=send, recv_sem=recv, device_id=to, device_id_type=MESH
        )
        made.start()
        sent.append(made)

    def arrived(dst, send, recv):
        pltpu.make_async_remote_copy(
            src_ref=dst,
            dst_ref=dst,
            send_sem=send,
            recv_sem=recv,
            device_id=(dp, lax.rem(me + 1, width)),
            device_id_type=MESH,
        ).wait_recv()

    sent = []
    in_quad = lambda k: (cls * QUAD + k, me)
    in_plane = lambda off: (dp, lax.rem(me + off, width))
    anyone = lambda a, b: (lax.rem(dp + a * QUAD, groups), lax.rem(me + b, width))
    in_class = lambda off: anyone(off, 0)

    loads = [
        pltpu.make_async_copy(src, dst, local_sems.at[j])
        for j, (src, dst) in enumerate(
            (
                (idx_hbm, idx_ref),
                (cnt_hbm, cnt_ref),
                (pts_hbm, pts.at[mine]),
                (fc_hbm, fc_ref),
            )
        )
    ]
    for load in loads:
        load.start()
    barrier = pltpu.get_barrier_semaphore()
    for off in range(1, width):
        pl.semaphore_signal(barrier, inc=1, device_id=in_plane(off), device_id_type=MESH)
    for k in (partner, across, diagonal):
        pl.semaphore_signal(barrier, inc=1, device_id=in_quad(k), device_id_type=MESH)
    for a in range(1, classes):
        for b in range(width):
            pl.semaphore_signal(barrier, inc=1, device_id=anyone(a, b), device_id_type=MESH)

    def cross(j):
        span = pl.ds(j * chunk, chunk)
        copy(pts_hbm.at[span], pts.at[mine, span], z_send.at[j], z_recv.at[j], in_quad(across))

    pl.semaphore_wait(barrier, classes * width - 1 + QUAD - 1)
    for j in range(chunks - 1):
        cross(j)
    for load in loads[:3]:
        load.wait()
    spot = lax.broadcasted_iota(jnp.int32, (rows, total), 0)
    slot = lax.broadcasted_iota(jnp.int32, (rows, total), 1)
    hits = [(spot == idx_ref[t, 0]) & (slot < cnt_ref[t]) for t in range(rounds)]
    chosen = lax.dot_general(
        jnp.concatenate([jnp.where(hit, 1.0, 0.0) for hit in hits], axis=1).astype(pts.dtype),
        pts[mine],
        CONTRACT_FIRST,
        preferred_element_type=jnp.float32,
    ).astype(packed.dtype)
    for t in range(rounds):
        packed[:, t] = chosen[t * total : (t + 1) * total].reshape(width, each, depth)
    for off in range(1, width):
        copy(
            packed.at[lax.rem(me + off, width)],
            parts.at[me],
            part_send.at[off - 1],
            part_recv.at[off - 1],
            in_plane(off),
        )
    copy(pts_hbm, pts.at[mine], core_send, core_recv, in_quad(partner))

    squares = jnp.square(pts[mine].astype(jnp.float32))
    lanes = squares[:, :LANES]
    for j in range(1, depth // LANES):
        lanes = lanes + squares[:, j * LANES : (j + 1) * LANES]
    rows_norm = jnp.sum(lanes.T, axis=0, keepdims=True)
    loads[3].wait()
    first = fc_ref[...].reshape(1, depth)
    first_norm = jnp.sum(jnp.square(first.astype(jnp.float32)), axis=1, keepdims=True)
    first_prod = lax.dot_general(
        jnp.broadcast_to(first, (TILE_ROWS, depth)),
        pts[mine],
        CONTRACT_LAST,
        preferred_element_type=jnp.float32,
    )[:1]
    running = jnp.maximum(rows_norm + first_norm - 2.0 * first_prod, 0.0)

    def spread(c, at):
        for off in range(1, width):
            copy(
                cand.at[c, me],
                cand.at[c, me],
                plane_send.at[at, off - 1],
                plane_recv.at[at, off - 1],
                in_plane(off),
            )

    held = packed[me].astype(jnp.float32)
    for off in range(1, width):
        source = lax.rem(me - off + width, width)
        arrived(parts.at[source], part_send.at[off - 1], part_recv.at[off - 1])
        held = held + parts[source].astype(jnp.float32)
    cand[cls, me] = held.astype(cand.dtype)
    for off in range(1, classes):
        copy(
            cand.at[cls, me],
            cand.at[cls, me],
            class_send.at[off - 1],
            class_recv.at[off - 1],
            in_class(off),
        )
    spread(cls, 0)
    cross(chunks - 1)
    for off in range(1, classes):
        source = lax.rem(cls - off + classes, classes)
        arrived(cand.at[source, me], class_send.at[off - 1], class_recv.at[off - 1])
        spread(source, off)

    def forward(j):
        span = pl.ds(j * chunk, chunk)
        arrived(pts.at[across, span], z_send.at[j], z_recv.at[j])
        copy(
            pts.at[across, span], pts.at[across, span], fwd_send.at[j], fwd_recv.at[j], in_quad(partner)
        )

    for j in range(chunks - 1):
        forward(j)

    def centers(c):
        return cand[c].reshape(width * rounds * each, depth)

    def center_norms(c):
        return jnp.sum(jnp.square(centers(c).astype(jnp.float32)), axis=1, keepdims=True)

    def least(c, norms, k, lo, size):
        prod = lax.dot_general(
            centers(c), pts[k, lo : lo + size], CONTRACT_LAST, preferred_element_type=jnp.float32
        )
        dist = (norms - 2.0 * prod).reshape(width, rounds, each, size)
        return jnp.min(jnp.min(dist, axis=0), axis=1)

    tall = least_out.shape[0]
    least_out[QUAD * rounds :] = jnp.concatenate(
        [rows_norm, running]
        + [jnp.zeros_like(running)] * (tall - QUAD * rounds - 2),
        axis=0,
    )
    turn = [lax.rem(cls - at + classes, classes) for at in range(classes)]
    found = {}
    for at, c in enumerate(turn):
        for off in range(1, width):
            source = lax.rem(me - off + width, width)
            arrived(cand.at[c, source], plane_send.at[at, off - 1], plane_recv.at[at, off - 1])
        norms = center_norms(c)
        for name, k in enumerate((mine, partner, across, diagonal)):
            if at == 0 and name == 1:
                arrived(pts.at[partner], core_send, core_recv)
            if at == 0 and name == 2:
                forward(chunks - 1)
            if at == 0 and name == 3:
                for j in range(chunks):
                    span = pl.ds(j * chunk, chunk)
                    arrived(pts.at[diagonal, span], fwd_send.at[j], fwd_recv.at[j])
            this = least(c, norms, k, 0, rows)
            found[name] = this if at == 0 else jnp.minimum(found[name], this)
            if at == classes - 1:
                least_out[name * rounds : (name + 1) * rounds] = found[name]

    for at, k in enumerate((partner, across, diagonal)):
        copy(least_out, least_in.at[at], least_send.at[at], least_recv.at[at], in_quad(k))
    told = [least_out[...]]
    for at in range(QUAD - 1):
        arrived(least_in.at[at], least_send.at[at], least_recv.at[at])
        told.append(least_in[at])

    def fold(row):
        out = row[:, :LANES]
        for j in range(1, rows // LANES):
            out = out + row[:, j * LANES : (j + 1) * LANES]
        return out

    def block_rows(block):
        near = told[block][0:rounds]
        for at in range(QUAD):
            if at == block:
                continue
            from_row = (at ^ block) * rounds
            near = jnp.minimum(near, told[at][from_row : from_row + rounds])
        norm = told[block][QUAD * rounds : QUAD * rounds + 1]
        steps = [told[block][QUAD * rounds + 1 : QUAD * rounds + 2]]
        for t in range(rounds):
            steps.append(jnp.minimum(steps[-1], jnp.maximum(norm + near[t : t + 1], 0.0)))
        return steps

    blocks = [block_rows(block) for block in range(QUAD)]
    running = blocks[0][-1]
    run_ref[...] = running
    partials = [
        (fold(blocks[0][t]) + fold(blocks[1][t])) + (fold(blocks[2][t]) + fold(blocks[3][t]))
        for t in range(rounds + 1)
    ]
    partials += [jnp.zeros_like(partials[0])] * (all_sums.shape[2] - len(partials))
    all_sums[cls, me] = jnp.concatenate(partials, axis=0)
    others = [(a, b) for a in range(classes) for b in range(width) if a or b]
    for a, b in others:
        copy(
            all_sums.at[cls, me],
            all_sums.at[cls, me],
            sum_send.at[a, b],
            sum_recv.at[a, b],
            anyone(a, b),
        )
    for a, b in others:
        source = (lax.rem(cls - a + classes, classes), lax.rem(me - b + width, width))
        arrived(all_sums.at[source], sum_send.at[a, b], sum_recv.at[a, b])
    sums = jnp.sum(
        jnp.sum(all_sums[...].reshape(classes * width, all_sums.shape[2], LANES), axis=0),
        axis=1,
        keepdims=True,
    )
    rows_all = rows * groups * width
    wgt_ref[...] = running * (rows_all / sums[rounds : rounds + 1])
    for t in range(rounds + 1):
        pot_ref[t] = sums[t, 0]
    for made in sent:
        made.wait_send()


def hand_on(*refs):
    *arrays, sems = refs
    count = len(arrays) // 2
    copies = [
        pltpu.make_async_copy(arrays[j], arrays[count + j], sems.at[j]) for j in range(count)
    ]
    for each in copies:
        each.start()
    for each in copies:
        each.wait()


def fused(points, first_center, counts, cand_index):
    rows, depth = points.shape
    rounds, total = counts.shape[0], cand_index.shape[3]
    groups, width = lax.axis_size("dp"), lax.axis_size("shard")
    each, classes = total // width, groups // QUAD
    chunks, tall = 4, (QUAD * rounds + 2 + 7) // 8 * 8
    f32, held = jnp.float32, points.dtype
    dma = pltpu.SemaphoreType.DMA
    vmem = pl.BlockSpec(memory_space=pltpu.VMEM)
    hbm = pl.BlockSpec(memory_space=pltpu.HBM)
    running, weights, potentials = pl.pallas_call(
        functools.partial(round_kernel, groups, width),
        out_shape=(
            jax.ShapeDtypeStruct((1, rows), f32),
            jax.ShapeDtypeStruct((1, rows), f32),
            jax.ShapeDtypeStruct((rounds + 1,), f32),
        ),
        in_specs=[hbm] * 4,
        out_specs=(vmem, vmem, pl.BlockSpec(memory_space=pltpu.SMEM)),
        scratch_shapes=[
            pltpu.VMEM((depth,), held),
            pltpu.SMEM((rounds,), counts.dtype),
            pltpu.VMEM(cand_index.shape, cand_index.dtype),
            pltpu.VMEM((QUAD, rows, depth), held),
            pltpu.VMEM((width, rounds, each, depth), held),
            pltpu.VMEM((width, rounds, each, depth), held),
            pltpu.VMEM((classes, width, rounds, each, depth), held),
            pltpu.VMEM((tall, rows), f32),
            pltpu.VMEM((QUAD - 1, tall, rows), f32),
            pltpu.VMEM((classes, width, 8, LANES), f32),
            dma((4,)),
            dma((width - 1,)),
            dma((width - 1,)),
            dma((classes, width - 1)),
            dma((classes, width - 1)),
            dma((max(classes - 1, 1),)),
            dma((max(classes - 1, 1),)),
            dma,
            dma,
            dma((chunks,)),
            dma((chunks,)),
            dma((chunks,)),
            dma((chunks,)),
            dma((QUAD - 1,)),
            dma((QUAD - 1,)),
            dma((classes, width)),
            dma((classes, width)),
        ],
        compiler_params=pltpu.CompilerParams(
            collective_id=0, has_side_effects=True, vmem_limit_bytes=VMEM_GRANT
        ),
    )(
        points,
        first_center,
        counts.reshape(rounds),
        cand_index,
    )
    made = (running.reshape(rows), weights.reshape(rows), potentials)
    return pl.pallas_call(
        hand_on,
        out_shape=[jax.ShapeDtypeStruct(part.shape, part.dtype) for part in made],
        in_specs=[hbm] * len(made),
        out_specs=[hbm] * len(made),
        scratch_shapes=[dma((len(made),))],
        compiler_params=pltpu.CompilerParams(vmem_limit_bytes=VMEM_GRANT),
    )(*made)


def one_holder(points, counts, cand_index):
    rows, depth = points.shape
    groups, width = lax.axis_size("dp"), lax.axis_size("shard")
    total = CANDS_ALL // groups
    return (
        cand_index.shape[3] == total
        and groups % QUAD == 0
        and width > 1
        and total % (width * TILE_ROWS) == 0
        and rows % (2 * LANES) == 0
        and depth % LANES == 0
        and counts.shape[0] < 8
    )


def pair_dist(rows, rows_norm, cands):
    prod = jnp.dot(rows, cands.T, preferred_element_type=jnp.float32)
    cand_norm = jnp.sum(jnp.square(cands.astype(jnp.float32)), axis=1)
    return jnp.maximum(rows_norm[:, None] + cand_norm[None, :] - 2.0 * prod, 0.0)


def pack_group(group_rows, member_counts, total, stride):
    ends = jnp.cumsum(member_counts)
    begins = ends - member_counts
    slot = jnp.arange(total, dtype=jnp.int32)
    source = jnp.sum((slot[:, None] >= ends[None, :]).astype(jnp.int32), axis=1)
    offset = slot - jnp.take(begins, source)
    return jnp.take(group_rows, source * stride + offset, axis=0)


def separate(points, first_center, counts, cand_index):
    rows_norm = jnp.sum(jnp.square(points.astype(jnp.float32)), axis=1)
    running = jnp.min(pair_dist(points, rows_norm, first_center[None, :]), axis=1)
    rounds = counts.shape[0]
    cap = cand_index.shape[3]
    every_count = lax.all_gather(counts.reshape(rounds, 1), ("dp", "shard"), axis=1, tiled=True)

    def global_sum(value):
        return lax.psum(value, ("dp", "shard"))

    partials = [jnp.sum(running)]
    totals = [global_sum(partials[0])]
    for step in range(rounds):
        local_rows = jnp.take(points, cand_index[step, 0, 0], axis=0)
        group_rows = lax.all_gather(local_rows, "shard", axis=0, tiled=True)
        width = lax.axis_size("shard")
        member_counts = lax.dynamic_slice_in_dim(
            every_count[step], lax.axis_index("dp") * width, width
        )
        total = CANDS_ALL // lax.axis_size("dp")
        packed = pack_group(group_rows, member_counts, total, cap)
        running = jnp.minimum(
            running,
            jnp.min(
                pair_dist(points, rows_norm, lax.all_gather(packed, "dp", axis=0, tiled=True)),
                axis=1,
            ),
        )
        partials.append(jnp.sum(running))
        totals.append(global_sum(partials[-1]))
    potentials = jnp.stack(totals)
    rows_total = points.shape[0] * lax.axis_size("dp") * lax.axis_size("shard")
    weights = running * (rows_total / potentials[-1])
    return (running, weights, potentials)


def body(points, first_center, counts, cand_index):
    if one_holder(points, counts, cand_index):
        return fused(points, first_center, counts, cand_index)
    return separate(points, first_center, counts, cand_index)


def solution(mesh):
    placed = (P(("dp", "shard"), None), P(), P(None, "dp", "shard"), P(None, "dp", "shard", None))
    return jax.shard_map(
        body,
        mesh=mesh,
        in_specs=placed,
        out_specs=(P(("dp", "shard")), P(("dp", "shard")), P()),
        check_vma=False,
    )
```

```python
import functools

import jax
import jax.numpy as jnp
from jax import lax
from jax.experimental import pallas as pl
from jax.experimental.pallas import tpu as pltpu
from jax.sharding import PartitionSpec as P

CANDS_ALL = 512
QUAD = 4
TILE_ROWS = 16
LANES = 128
VMEM_GRANT = 62 * 1024 * 1024
MESH = pl.DeviceIdType.MESH
CONTRACT_LAST = (((1,), (1,)), ((), ()))
CONTRACT_FIRST = (((0,), (0,)), ((), ()))


def round_kernel(
    groups,
    width,
    pts_hbm,
    fc_hbm,
    cnt_hbm,
    idx_hbm,
    run_ref,
    wgt_ref,
    pot_ref,
    fc_ref,
    cnt_ref,
    idx_ref,
    pts,
    packed,
    parts,
    cand,
    least_out,
    least_in,
    all_sums,
    local_sems,
    part_send,
    part_recv,
    plane_send,
    plane_recv,
    class_send,
    class_recv,
    core_send,
    core_recv,
    z_send,
    z_recv,
    fwd_send,
    fwd_recv,
    least_send,
    least_recv,
    sum_send,
    sum_recv,
):
    rounds, total = idx_ref.shape[0], idx_ref.shape[3]
    rows, depth = pts_hbm.shape
    each = total // width
    classes = groups // QUAD
    chunks = z_send.shape[0]
    chunk = rows // chunks

    dp, me = lax.axis_index("dp"), lax.axis_index("shard")
    pieces = [(0, 1), (1, rounds)] if rounds > 1 else [(0, rounds)]
    cls, mine = dp // QUAD, dp % QUAD
    zside, core = mine // 2, mine % 2
    partner = zside * 2 + (1 - core)
    across = (1 - zside) * 2 + core
    diagonal = (1 - zside) * 2 + (1 - core)

    def copy(src, dst, send, recv, to):
        made = pltpu.make_async_remote_copy(
            src_ref=src, dst_ref=dst, send_sem=send, recv_sem=recv, device_id=to, device_id_type=MESH
        )
        made.start()
        sent.append(made)

    def arrived(dst, send, recv):
        pltpu.make_async_remote_copy(
            src_ref=dst,
            dst_ref=dst,
            send_sem=send,
            recv_sem=recv,
            device_id=(dp, lax.rem(me + 1, width)),
            device_id_type=MESH,
        ).wait_recv()

    sent = []
    in_quad = lambda k: (cls * QUAD + k, me)
    in_plane = lambda off: (dp, lax.rem(me + off, width))
    anyone = lambda a, b: (lax.rem(dp + a * QUAD, groups), lax.rem(me + b, width))
    in_class = lambda off: anyone(off, 0)

    loads = [
        pltpu.make_async_copy(src, dst, local_sems.at[j])
        for j, (src, dst) in enumerate(
            (
                (idx_hbm, idx_ref),
                (cnt_hbm, cnt_ref),
                (pts_hbm, pts.at[mine]),
                (fc_hbm, fc_ref),
            )
        )
    ]
    for load in loads:
        load.start()
    barrier = pltpu.get_barrier_semaphore()
    for off in range(1, width):
        pl.semaphore_signal(barrier, inc=1, device_id=in_plane(off), device_id_type=MESH)
    for k in (partner, across, diagonal):
        pl.semaphore_signal(barrier, inc=1, device_id=in_quad(k), device_id_type=MESH)
    for a in range(1, classes):
        for b in range(width):
            pl.semaphore_signal(barrier, inc=1, device_id=anyone(a, b), device_id_type=MESH)

    def cross(j):
        span = pl.ds(j * chunk, chunk)
        copy(pts_hbm.at[span], pts.at[mine, span], z_send.at[j], z_recv.at[j], in_quad(across))

    pl.semaphore_wait(barrier, classes * width - 1 + QUAD - 1)
    early = chunks - len(pieces)
    for j in range(early):
        cross(j)
    for load in loads[:3]:
        load.wait()
    spot = lax.broadcasted_iota(jnp.int32, (rows, total), 0)
    slot = lax.broadcasted_iota(jnp.int32, (rows, total), 1)
    for p, (t0, t1) in enumerate(pieces):
        hits = [(spot == idx_ref[t, 0]) & (slot < cnt_ref[t]) for t in range(t0, t1)]
        chosen = lax.dot_general(
            jnp.concatenate([jnp.where(hit, 1.0, 0.0) for hit in hits], axis=1).astype(pts.dtype),
            pts[mine],
            CONTRACT_FIRST,
            preferred_element_type=jnp.float32,
        ).astype(packed.dtype)
        for t in range(t0, t1):
            at = (t - t0) * total
            packed[:, t] = chosen[at : at + total].reshape(width, each, depth)
        for off in range(1, width):
            copy(
                packed.at[lax.rem(me + off, width), t0:t1],
                parts.at[me, t0:t1],
                part_send.at[p, off - 1],
                part_recv.at[p, off - 1],
                in_plane(off),
            )
    copy(pts_hbm, pts.at[mine], core_send, core_recv, in_quad(partner))

    squares = jnp.square(pts[mine].astype(jnp.float32))
    lanes = squares[:, :LANES]
    for j in range(1, depth // LANES):
        lanes = lanes + squares[:, j * LANES : (j + 1) * LANES]
    rows_norm = jnp.sum(lanes.T, axis=0, keepdims=True)
    loads[3].wait()
    first = fc_ref[...].reshape(1, depth)
    first_norm = jnp.sum(jnp.square(first.astype(jnp.float32)), axis=1, keepdims=True)
    first_prod = lax.dot_general(
        jnp.broadcast_to(first, (TILE_ROWS, depth)),
        pts[mine],
        CONTRACT_LAST,
        preferred_element_type=jnp.float32,
    )[:1]
    running = jnp.maximum(rows_norm + first_norm - 2.0 * first_prod, 0.0)

    def spread(c, at, p):
        t0, t1 = pieces[p]
        for off in range(1, width):
            copy(
                cand.at[c, me, t0:t1],
                cand.at[c, me, t0:t1],
                plane_send.at[at, p, off - 1],
                plane_recv.at[at, p, off - 1],
                in_plane(off),
            )

    for p, (t0, t1) in enumerate(pieces):
        held = packed[me, t0:t1].astype(jnp.float32)
        for off in range(1, width):
            source = lax.rem(me - off + width, width)
            arrived(parts.at[source, t0:t1], part_send.at[p, off - 1], part_recv.at[p, off - 1])
            held = held + parts[source, t0:t1].astype(jnp.float32)
        cand[cls, me, t0:t1] = held.astype(cand.dtype)
        for off in range(1, classes):
            copy(
                cand.at[cls, me, t0:t1],
                cand.at[cls, me, t0:t1],
                class_send.at[p, off - 1],
                class_recv.at[p, off - 1],
                in_class(off),
            )
        spread(cls, 0, p)
        cross(early + p)
    for p, (t0, t1) in enumerate(pieces):
        for off in range(1, classes):
            source = lax.rem(cls - off + classes, classes)
            arrived(
                cand.at[source, me, t0:t1], class_send.at[p, off - 1], class_recv.at[p, off - 1]
            )
            spread(source, off, p)

    def forward(j):
        span = pl.ds(j * chunk, chunk)
        arrived(pts.at[across, span], z_send.at[j], z_recv.at[j])
        copy(
            pts.at[across, span], pts.at[across, span], fwd_send.at[j], fwd_recv.at[j], in_quad(partner)
        )

    for j in range(chunks - 1):
        forward(j)

    def centers(c):
        return cand[c].reshape(width * rounds * each, depth)

    def center_norms(c):
        return jnp.sum(jnp.square(centers(c).astype(jnp.float32)), axis=1, keepdims=True)

    def least(c, norms, k, lo, size):
        prod = lax.dot_general(
            centers(c), pts[k, lo : lo + size], CONTRACT_LAST, preferred_element_type=jnp.float32
        )
        dist = (norms - 2.0 * prod).reshape(width, rounds, each, size)
        return jnp.min(jnp.min(dist, axis=0), axis=1)

    tall = least_out.shape[0]
    least_out[QUAD * rounds :] = jnp.concatenate(
        [rows_norm, running]
        + [jnp.zeros_like(running)] * (tall - QUAD * rounds - 2),
        axis=0,
    )
    turn = [lax.rem(cls - at + classes, classes) for at in range(classes)]
    found = {}
    for at, c in enumerate(turn):
        for off in range(1, width):
            source = lax.rem(me - off + width, width)
            for p, (t0, t1) in enumerate(pieces):
                arrived(
                    cand.at[c, source, t0:t1],
                    plane_send.at[at, p, off - 1],
                    plane_recv.at[at, p, off - 1],
                )
        norms = center_norms(c)
        for name, k in enumerate((mine, partner, across, diagonal)):
            if at == 0 and name == 1:
                arrived(pts.at[partner], core_send, core_recv)
            if at == 0 and name == 2:
                forward(chunks - 1)
            if at == 0 and name == 3:
                for j in range(chunks):
                    span = pl.ds(j * chunk, chunk)
                    arrived(pts.at[diagonal, span], fwd_send.at[j], fwd_recv.at[j])
            this = least(c, norms, k, 0, rows)
            found[name] = this if at == 0 else jnp.minimum(found[name], this)
            if at == classes - 1:
                least_out[name * rounds : (name + 1) * rounds] = found[name]

    for at, k in enumerate((partner, across, diagonal)):
        copy(least_out, least_in.at[at], least_send.at[at], least_recv.at[at], in_quad(k))
    told = [least_out[...]]
    for at in range(QUAD - 1):
        arrived(least_in.at[at], least_send.at[at], least_recv.at[at])
        told.append(least_in[at])

    def fold(row):
        out = row[:, :LANES]
        for j in range(1, rows // LANES):
            out = out + row[:, j * LANES : (j + 1) * LANES]
        return out

    def block_rows(block):
        near = told[block][0:rounds]
        for at in range(QUAD):
            if at == block:
                continue
            from_row = (at ^ block) * rounds
            near = jnp.minimum(near, told[at][from_row : from_row + rounds])
        norm = told[block][QUAD * rounds : QUAD * rounds + 1]
        steps = [told[block][QUAD * rounds + 1 : QUAD * rounds + 2]]
        for t in range(rounds):
            steps.append(jnp.minimum(steps[-1], jnp.maximum(norm + near[t : t + 1], 0.0)))
        return steps

    blocks = [block_rows(block) for block in range(QUAD)]
    running = blocks[0][-1]
    run_ref[...] = running
    partials = [
        (fold(blocks[0][t]) + fold(blocks[1][t])) + (fold(blocks[2][t]) + fold(blocks[3][t]))
        for t in range(rounds + 1)
    ]
    partials += [jnp.zeros_like(partials[0])] * (all_sums.shape[2] - len(partials))
    all_sums[cls, me] = jnp.concatenate(partials, axis=0)
    others = [(a, b) for a in range(classes) for b in range(width) if a or b]
    for a, b in others:
        copy(
            all_sums.at[cls, me],
            all_sums.at[cls, me],
            sum_send.at[a, b],
            sum_recv.at[a, b],
            anyone(a, b),
        )
    for a, b in others:
        source = (lax.rem(cls - a + classes, classes), lax.rem(me - b + width, width))
        arrived(all_sums.at[source], sum_send.at[a, b], sum_recv.at[a, b])
    sums = jnp.sum(
        jnp.sum(all_sums[...].reshape(classes * width, all_sums.shape[2], LANES), axis=0),
        axis=1,
        keepdims=True,
    )
    rows_all = rows * groups * width
    wgt_ref[...] = running * (rows_all / sums[rounds : rounds + 1])
    for t in range(rounds + 1):
        pot_ref[t] = sums[t, 0]
    for made in sent:
        made.wait_send()


def hand_on(*refs):
    *arrays, sems = refs
    count = len(arrays) // 2
    copies = [
        pltpu.make_async_copy(arrays[j], arrays[count + j], sems.at[j]) for j in range(count)
    ]
    for each in copies:
        each.start()
    for each in copies:
        each.wait()


def fused(points, first_center, counts, cand_index):
    rows, depth = points.shape
    rounds, total = counts.shape[0], cand_index.shape[3]
    groups, width = lax.axis_size("dp"), lax.axis_size("shard")
    each, classes = total // width, groups // QUAD
    chunks, tall = 4, (QUAD * rounds + 2 + 7) // 8 * 8
    f32, held = jnp.float32, points.dtype
    dma = pltpu.SemaphoreType.DMA
    vmem = pl.BlockSpec(memory_space=pltpu.VMEM)
    hbm = pl.BlockSpec(memory_space=pltpu.HBM)
    running, weights, potentials = pl.pallas_call(
        functools.partial(round_kernel, groups, width),
        out_shape=(
            jax.ShapeDtypeStruct((1, rows), f32),
            jax.ShapeDtypeStruct((1, rows), f32),
            jax.ShapeDtypeStruct((rounds + 1,), f32),
        ),
        in_specs=[hbm] * 4,
        out_specs=(vmem, vmem, pl.BlockSpec(memory_space=pltpu.SMEM)),
        scratch_shapes=[
            pltpu.VMEM((depth,), held),
            pltpu.SMEM((rounds,), counts.dtype),
            pltpu.VMEM(cand_index.shape, cand_index.dtype),
            pltpu.VMEM((QUAD, rows, depth), held),
            pltpu.VMEM((width, rounds, each, depth), held),
            pltpu.VMEM((width, rounds, each, depth), held),
            pltpu.VMEM((classes, width, rounds, each, depth), held),
            pltpu.VMEM((tall, rows), f32),
            pltpu.VMEM((QUAD - 1, tall, rows), f32),
            pltpu.VMEM((classes, width, 8, LANES), f32),
            dma((4,)),
            dma((2, width - 1)),
            dma((2, width - 1)),
            dma((classes, 2, width - 1)),
            dma((classes, 2, width - 1)),
            dma((2, max(classes - 1, 1))),
            dma((2, max(classes - 1, 1))),
            dma,
            dma,
            dma((chunks,)),
            dma((chunks,)),
            dma((chunks,)),
            dma((chunks,)),
            dma((QUAD - 1,)),
            dma((QUAD - 1,)),
            dma((classes, width)),
            dma((classes, width)),
        ],
        compiler_params=pltpu.CompilerParams(
            collective_id=0, has_side_effects=True, vmem_limit_bytes=VMEM_GRANT
        ),
    )(
        points,
        first_center,
        counts.reshape(rounds),
        cand_index,
    )
    made = (running.reshape(rows), weights.reshape(rows), potentials)
    return pl.pallas_call(
        hand_on,
        out_shape=[jax.ShapeDtypeStruct(part.shape, part.dtype) for part in made],
        in_specs=[hbm] * len(made),
        out_specs=[hbm] * len(made),
        scratch_shapes=[dma((len(made),))],
        compiler_params=pltpu.CompilerParams(vmem_limit_bytes=VMEM_GRANT),
    )(*made)


def one_holder(points, counts, cand_index):
    rows, depth = points.shape
    groups, width = lax.axis_size("dp"), lax.axis_size("shard")
    total = CANDS_ALL // groups
    return (
        cand_index.shape[3] == total
        and groups % QUAD == 0
        and width > 1
        and total % (width * TILE_ROWS) == 0
        and rows % (2 * LANES) == 0
        and depth % LANES == 0
        and counts.shape[0] < 8
    )


def pair_dist(rows, rows_norm, cands):
    prod = jnp.dot(rows, cands.T, preferred_element_type=jnp.float32)
    cand_norm = jnp.sum(jnp.square(cands.astype(jnp.float32)), axis=1)
    return jnp.maximum(rows_norm[:, None] + cand_norm[None, :] - 2.0 * prod, 0.0)


def pack_group(group_rows, member_counts, total, stride):
    ends = jnp.cumsum(member_counts)
    begins = ends - member_counts
    slot = jnp.arange(total, dtype=jnp.int32)
    source = jnp.sum((slot[:, None] >= ends[None, :]).astype(jnp.int32), axis=1)
    offset = slot - jnp.take(begins, source)
    return jnp.take(group_rows, source * stride + offset, axis=0)


def separate(points, first_center, counts, cand_index):
    rows_norm = jnp.sum(jnp.square(points.astype(jnp.float32)), axis=1)
    running = jnp.min(pair_dist(points, rows_norm, first_center[None, :]), axis=1)
    rounds = counts.shape[0]
    cap = cand_index.shape[3]
    every_count = lax.all_gather(counts.reshape(rounds, 1), ("dp", "shard"), axis=1, tiled=True)

    def global_sum(value):
        return lax.psum(value, ("dp", "shard"))

    partials = [jnp.sum(running)]
    totals = [global_sum(partials[0])]
    for step in range(rounds):
        local_rows = jnp.take(points, cand_index[step, 0, 0], axis=0)
        group_rows = lax.all_gather(local_rows, "shard", axis=0, tiled=True)
        width = lax.axis_size("shard")
        member_counts = lax.dynamic_slice_in_dim(
            every_count[step], lax.axis_index("dp") * width, width
        )
        total = CANDS_ALL // lax.axis_size("dp")
        packed = pack_group(group_rows, member_counts, total, cap)
        running = jnp.minimum(
            running,
            jnp.min(
                pair_dist(points, rows_norm, lax.all_gather(packed, "dp", axis=0, tiled=True)),
                axis=1,
            ),
        )
        partials.append(jnp.sum(running))
        totals.append(global_sum(partials[-1]))
    potentials = jnp.stack(totals)
    rows_total = points.shape[0] * lax.axis_size("dp") * lax.axis_size("shard")
    weights = running * (rows_total / potentials[-1])
    return (running, weights, potentials)


def body(points, first_center, counts, cand_index):
    if one_holder(points, counts, cand_index):
        return fused(points, first_center, counts, cand_index)
    return separate(points, first_center, counts, cand_index)


def solution(mesh):
    placed = (P(("dp", "shard"), None), P(), P(None, "dp", "shard"), P(None, "dp", "shard", None))
    return jax.shard_map(
        body,
        mesh=mesh,
        in_specs=placed,
        out_specs=(P(("dp", "shard")), P(("dp", "shard")), P()),
        check_vma=False,
    )
```

```python
import functools

import jax
import jax.numpy as jnp
from jax import lax
from jax.experimental import pallas as pl
from jax.experimental.pallas import tpu as pltpu
from jax.sharding import PartitionSpec as P

CANDS_ALL = 512
QUAD = 4
TILE_ROWS = 16
LANES = 128
VMEM_GRANT = 62 * 1024 * 1024
MESH = pl.DeviceIdType.MESH
CONTRACT_LAST = (((1,), (1,)), ((), ()))
CONTRACT_FIRST = (((0,), (0,)), ((), ()))


def round_kernel(
    groups,
    width,
    pts_hbm,
    fc_hbm,
    cnt_hbm,
    idx_hbm,
    run_hbm,
    wgt_hbm,
    pot_hbm,
    run_ref,
    wgt_ref,
    pot_ref,
    fc_ref,
    cnt_ref,
    idx_ref,
    pts,
    packed,
    parts,
    cand,
    least_out,
    least_in,
    all_sums,
    local_sems,
    out_sems,
    part_send,
    part_recv,
    plane_send,
    plane_recv,
    class_send,
    class_recv,
    core_send,
    core_recv,
    z_send,
    z_recv,
    fwd_send,
    fwd_recv,
    least_send,
    least_recv,
    sum_send,
    sum_recv,
):
    rounds, total = idx_ref.shape[0], idx_ref.shape[3]
    rows, depth = pts_hbm.shape
    each = total // width
    classes = groups // QUAD
    chunks = z_send.shape[0]
    chunk = rows // chunks

    dp, me = lax.axis_index("dp"), lax.axis_index("shard")
    pieces = [(0, 1), (1, rounds)] if rounds > 1 else [(0, rounds)]
    cls, mine = dp // QUAD, dp % QUAD
    zside, core = mine // 2, mine % 2
    partner = zside * 2 + (1 - core)
    across = (1 - zside) * 2 + core
    diagonal = (1 - zside) * 2 + (1 - core)

    def copy(src, dst, send, recv, to):
        made = pltpu.make_async_remote_copy(
            src_ref=src, dst_ref=dst, send_sem=send, recv_sem=recv, device_id=to, device_id_type=MESH
        )
        made.start()
        sent.append(made)

    def arrived(dst, send, recv):
        pltpu.make_async_remote_copy(
            src_ref=dst,
            dst_ref=dst,
            send_sem=send,
            recv_sem=recv,
            device_id=(dp, lax.rem(me + 1, width)),
            device_id_type=MESH,
        ).wait_recv()

    sent = []
    in_quad = lambda k: (cls * QUAD + k, me)
    in_plane = lambda off: (dp, lax.rem(me + off, width))
    anyone = lambda a, b: (lax.rem(dp + a * QUAD, groups), lax.rem(me + b, width))
    in_class = lambda off: anyone(off, 0)

    loads = [
        pltpu.make_async_copy(src, dst, local_sems.at[j])
        for j, (src, dst) in enumerate(
            (
                (idx_hbm, idx_ref),
                (cnt_hbm, cnt_ref),
                (pts_hbm, pts.at[mine]),
                (fc_hbm, fc_ref),
            )
        )
    ]
    for load in loads:
        load.start()
    barrier = pltpu.get_barrier_semaphore()
    for off in range(1, width):
        pl.semaphore_signal(barrier, inc=1, device_id=in_plane(off), device_id_type=MESH)
    for k in (partner, across, diagonal):
        pl.semaphore_signal(barrier, inc=1, device_id=in_quad(k), device_id_type=MESH)
    for a in range(1, classes):
        for b in range(width):
            pl.semaphore_signal(barrier, inc=1, device_id=anyone(a, b), device_id_type=MESH)

    def cross(j):
        span = pl.ds(j * chunk, chunk)
        copy(pts_hbm.at[span], pts.at[mine, span], z_send.at[j], z_recv.at[j], in_quad(across))

    pl.semaphore_wait(barrier, classes * width - 1 + QUAD - 1)
    for j in range(chunks - 1):
        cross(j)
    for load in loads[:3]:
        load.wait()
    spot = lax.broadcasted_iota(jnp.int32, (rows, total), 0)
    slot = lax.broadcasted_iota(jnp.int32, (rows, total), 1)
    for p, (t0, t1) in enumerate(pieces):
        hits = [(spot == idx_ref[t, 0]) & (slot < cnt_ref[t]) for t in range(t0, t1)]
        chosen = lax.dot_general(
            jnp.concatenate([jnp.where(hit, 1.0, 0.0) for hit in hits], axis=1).astype(pts.dtype),
            pts[mine],
            CONTRACT_FIRST,
            preferred_element_type=jnp.float32,
        ).astype(packed.dtype)
        for t in range(t0, t1):
            at = (t - t0) * total
            packed[:, t] = chosen[at : at + total].reshape(width, each, depth)
        for off in range(1, width):
            copy(
                packed.at[lax.rem(me + off, width), t0:t1],
                parts.at[me, t0:t1],
                part_send.at[p, off - 1],
                part_recv.at[p, off - 1],
                in_plane(off),
            )
    copy(pts_hbm, pts.at[mine], core_send, core_recv, in_quad(partner))

    squares = jnp.square(pts[mine].astype(jnp.float32))
    lanes = squares[:, :LANES]
    for j in range(1, depth // LANES):
        lanes = lanes + squares[:, j * LANES : (j + 1) * LANES]
    rows_norm = jnp.sum(lanes.T, axis=0, keepdims=True)
    loads[3].wait()
    first = fc_ref[...].reshape(1, depth)
    first_norm = jnp.sum(jnp.square(first.astype(jnp.float32)), axis=1, keepdims=True)
    first_prod = lax.dot_general(
        jnp.broadcast_to(first, (TILE_ROWS, depth)),
        pts[mine],
        CONTRACT_LAST,
        preferred_element_type=jnp.float32,
    )[:1]
    running = jnp.maximum(rows_norm + first_norm - 2.0 * first_prod, 0.0)

    def spread(c, at, p):
        t0, t1 = pieces[p]
        for off in range(1, width):
            copy(
                cand.at[c, me, t0:t1],
                cand.at[c, me, t0:t1],
                plane_send.at[at, p, off - 1],
                plane_recv.at[at, p, off - 1],
                in_plane(off),
            )

    for p, (t0, t1) in enumerate(pieces):
        held = packed[me, t0:t1].astype(jnp.float32)
        for off in range(1, width):
            source = lax.rem(me - off + width, width)
            arrived(parts.at[source, t0:t1], part_send.at[p, off - 1], part_recv.at[p, off - 1])
            held = held + parts[source, t0:t1].astype(jnp.float32)
        cand[cls, me, t0:t1] = held.astype(cand.dtype)
        for off in range(1, classes):
            copy(
                cand.at[cls, me, t0:t1],
                cand.at[cls, me, t0:t1],
                class_send.at[p, off - 1],
                class_recv.at[p, off - 1],
                in_class(off),
            )
        spread(cls, 0, p)
    cross(chunks - 1)
    for p, (t0, t1) in enumerate(pieces):
        for off in range(1, classes):
            source = lax.rem(cls - off + classes, classes)
            arrived(
                cand.at[source, me, t0:t1], class_send.at[p, off - 1], class_recv.at[p, off - 1]
            )
            spread(source, off, p)

    def forward(j):
        span = pl.ds(j * chunk, chunk)
        arrived(pts.at[across, span], z_send.at[j], z_recv.at[j])
        copy(
            pts.at[across, span], pts.at[across, span], fwd_send.at[j], fwd_recv.at[j], in_quad(partner)
        )

    for j in range(chunks - 1):
        forward(j)

    def least(c, t0, t1, names):
        centers = cand[c, :, t0:t1].reshape(width * (t1 - t0) * each, depth)
        norms = jnp.sum(jnp.square(centers.astype(jnp.float32)), axis=1, keepdims=True)
        for name in names:
            if callable(name):
                name()
                continue
            prod = lax.dot_general(
                centers, pts[places[name]], CONTRACT_LAST, preferred_element_type=jnp.float32
            )
            dist = (norms - 2.0 * prod).reshape(width, t1 - t0, each, rows)
            this = jnp.min(jnp.min(dist, axis=0), axis=1)
            for t in range(t0, t1):
                row = this[t - t0 : t - t0 + 1]
                old = found.get((name, t))
                found[name, t] = row if old is None else jnp.minimum(old, row)

    def gathered(at, p):
        t0, t1 = pieces[p]
        c = lax.rem(cls - at + classes, classes)
        for off in range(1, width):
            source = lax.rem(me - off + width, width)
            arrived(
                cand.at[c, source, t0:t1],
                plane_send.at[at, p, off - 1],
                plane_recv.at[at, p, off - 1],
            )
        return c

    def across_ready():
        forward(chunks - 1)

    def diagonal_ready():
        for j in range(chunks):
            span = pl.ds(j * chunk, chunk)
            arrived(pts.at[diagonal, span], fwd_send.at[j], fwd_recv.at[j])

    places = (mine, partner, across, diagonal)
    found = {}
    tall = least_out.shape[0]
    least_out[QUAD * rounds :] = jnp.concatenate(
        [rows_norm, running]
        + [jnp.zeros_like(running)] * (tall - QUAD * rounds - 2),
        axis=0,
    )
    for p in range(len(pieces)):
        c = gathered(0, p)
    arrived(pts.at[partner], core_send, core_recv)
    least(c, 0, rounds, (0, 1, across_ready, 2, diagonal_ready, 3))
    for at in range(1, classes):
        for p, (t0, t1) in enumerate(pieces):
            c = gathered(at, p)
            least(c, t0, t1, range(QUAD))
    least_out[: QUAD * rounds] = jnp.concatenate(
        [found[name, t] for name in range(QUAD) for t in range(rounds)], axis=0
    )

    for at, k in enumerate((partner, across, diagonal)):
        copy(least_out, least_in.at[at], least_send.at[at], least_recv.at[at], in_quad(k))
    told = [least_out[...]]
    for at in range(QUAD - 1):
        arrived(least_in.at[at], least_send.at[at], least_recv.at[at])
        told.append(least_in[at])

    def fold(row):
        out = row[:, :LANES]
        for j in range(1, rows // LANES):
            out = out + row[:, j * LANES : (j + 1) * LANES]
        return out

    def block_rows(block):
        near = told[block][0:rounds]
        for at in range(QUAD):
            if at == block:
                continue
            from_row = (at ^ block) * rounds
            near = jnp.minimum(near, told[at][from_row : from_row + rounds])
        norm = told[block][QUAD * rounds : QUAD * rounds + 1]
        steps = [told[block][QUAD * rounds + 1 : QUAD * rounds + 2]]
        for t in range(rounds):
            steps.append(jnp.minimum(steps[-1], jnp.maximum(norm + near[t : t + 1], 0.0)))
        return steps

    blocks = [block_rows(block) for block in range(QUAD)]
    running = blocks[0][-1]
    run_ref[...] = running
    leaving = [
        pltpu.make_async_copy(src, dst, out_sems.at[j])
        for j, (src, dst) in enumerate(((run_ref, run_hbm), (wgt_ref, wgt_hbm), (pot_ref, pot_hbm)))
    ]
    leaving[0].start()
    partials = [
        (fold(blocks[0][t]) + fold(blocks[1][t])) + (fold(blocks[2][t]) + fold(blocks[3][t]))
        for t in range(rounds + 1)
    ]
    partials += [jnp.zeros_like(partials[0])] * (all_sums.shape[2] - len(partials))
    all_sums[cls, me] = jnp.concatenate(partials, axis=0)
    others = [(a, b) for a in range(classes) for b in range(width) if a or b]
    for a, b in others:
        copy(
            all_sums.at[cls, me],
            all_sums.at[cls, me],
            sum_send.at[a, b],
            sum_recv.at[a, b],
            anyone(a, b),
        )
    for a, b in others:
        source = (lax.rem(cls - a + classes, classes), lax.rem(me - b + width, width))
        arrived(all_sums.at[source], sum_send.at[a, b], sum_recv.at[a, b])
    sums = jnp.sum(
        jnp.sum(all_sums[...].reshape(classes * width, all_sums.shape[2], LANES), axis=0),
        axis=1,
        keepdims=True,
    )
    rows_all = rows * groups * width
    wgt_ref[...] = running * (rows_all / sums[rounds : rounds + 1])
    for t in range(rounds + 1):
        pot_ref[t] = sums[t, 0]
    for made in leaving[1:]:
        made.start()
    for made in sent:
        made.wait_send()
    for made in leaving:
        made.wait()


def hand_on(*refs):
    *arrays, sems = refs
    count = len(arrays) // 2
    copies = [
        pltpu.make_async_copy(arrays[j], arrays[count + j], sems.at[j]) for j in range(count)
    ]
    for each in copies:
        each.start()
    for each in copies:
        each.wait()


def fused(points, first_center, counts, cand_index):
    rows, depth = points.shape
    rounds, total = counts.shape[0], cand_index.shape[3]
    groups, width = lax.axis_size("dp"), lax.axis_size("shard")
    each, classes = total // width, groups // QUAD
    chunks, tall = 4, (QUAD * rounds + 2 + 7) // 8 * 8
    f32, held = jnp.float32, points.dtype
    dma = pltpu.SemaphoreType.DMA
    hbm = pl.BlockSpec(memory_space=pltpu.HBM)
    running, weights, potentials = pl.pallas_call(
        functools.partial(round_kernel, groups, width),
        out_shape=(
            jax.ShapeDtypeStruct((1, rows), f32),
            jax.ShapeDtypeStruct((1, rows), f32),
            jax.ShapeDtypeStruct((rounds + 1,), f32),
        ),
        in_specs=[hbm] * 4,
        out_specs=[hbm] * 3,
        scratch_shapes=[
            pltpu.VMEM((1, rows), f32),
            pltpu.VMEM((1, rows), f32),
            pltpu.SMEM((rounds + 1,), f32),
            pltpu.VMEM((depth,), held),
            pltpu.SMEM((rounds,), counts.dtype),
            pltpu.VMEM(cand_index.shape, cand_index.dtype),
            pltpu.VMEM((QUAD, rows, depth), held),
            pltpu.VMEM((width, rounds, each, depth), held),
            pltpu.VMEM((width, rounds, each, depth), held),
            pltpu.VMEM((classes, width, rounds, each, depth), held),
            pltpu.VMEM((tall, rows), f32),
            pltpu.VMEM((QUAD - 1, tall, rows), f32),
            pltpu.VMEM((classes, width, 8, LANES), f32),
            dma((4,)),
            dma((3,)),
            dma((2, width - 1)),
            dma((2, width - 1)),
            dma((classes, 2, width - 1)),
            dma((classes, 2, width - 1)),
            dma((2, max(classes - 1, 1))),
            dma((2, max(classes - 1, 1))),
            dma,
            dma,
            dma((chunks,)),
            dma((chunks,)),
            dma((chunks,)),
            dma((chunks,)),
            dma((QUAD - 1,)),
            dma((QUAD - 1,)),
            dma((classes, width)),
            dma((classes, width)),
        ],
        compiler_params=pltpu.CompilerParams(
            collective_id=0, has_side_effects=True, vmem_limit_bytes=VMEM_GRANT
        ),
    )(
        points,
        first_center,
        counts.reshape(rounds),
        cand_index,
    )
    made = (running.reshape(rows), weights.reshape(rows), potentials)
    return pl.pallas_call(
        hand_on,
        out_shape=[jax.ShapeDtypeStruct(part.shape, part.dtype) for part in made],
        in_specs=[hbm] * len(made),
        out_specs=[hbm] * len(made),
        scratch_shapes=[dma((len(made),))],
        compiler_params=pltpu.CompilerParams(vmem_limit_bytes=VMEM_GRANT),
    )(*made)


def one_holder(points, counts, cand_index):
    rows, depth = points.shape
    groups, width = lax.axis_size("dp"), lax.axis_size("shard")
    total = CANDS_ALL // groups
    return (
        cand_index.shape[3] == total
        and groups % QUAD == 0
        and width > 1
        and total % (width * TILE_ROWS) == 0
        and rows % (2 * LANES) == 0
        and depth % LANES == 0
        and counts.shape[0] < 8
    )


def pair_dist(rows, rows_norm, cands):
    prod = jnp.dot(rows, cands.T, preferred_element_type=jnp.float32)
    cand_norm = jnp.sum(jnp.square(cands.astype(jnp.float32)), axis=1)
    return jnp.maximum(rows_norm[:, None] + cand_norm[None, :] - 2.0 * prod, 0.0)


def pack_group(group_rows, member_counts, total, stride):
    ends = jnp.cumsum(member_counts)
    begins = ends - member_counts
    slot = jnp.arange(total, dtype=jnp.int32)
    source = jnp.sum((slot[:, None] >= ends[None, :]).astype(jnp.int32), axis=1)
    offset = slot - jnp.take(begins, source)
    return jnp.take(group_rows, source * stride + offset, axis=0)


def separate(points, first_center, counts, cand_index):
    rows_norm = jnp.sum(jnp.square(points.astype(jnp.float32)), axis=1)
    running = jnp.min(pair_dist(points, rows_norm, first_center[None, :]), axis=1)
    rounds = counts.shape[0]
    cap = cand_index.shape[3]
    every_count = lax.all_gather(counts.reshape(rounds, 1), ("dp", "shard"), axis=1, tiled=True)

    def global_sum(value):
        return lax.psum(value, ("dp", "shard"))

    partials = [jnp.sum(running)]
    totals = [global_sum(partials[0])]
    for step in range(rounds):
        local_rows = jnp.take(points, cand_index[step, 0, 0], axis=0)
        group_rows = lax.all_gather(local_rows, "shard", axis=0, tiled=True)
        width = lax.axis_size("shard")
        member_counts = lax.dynamic_slice_in_dim(
            every_count[step], lax.axis_index("dp") * width, width
        )
        total = CANDS_ALL // lax.axis_size("dp")
        packed = pack_group(group_rows, member_counts, total, cap)
        running = jnp.minimum(
            running,
            jnp.min(
                pair_dist(points, rows_norm, lax.all_gather(packed, "dp", axis=0, tiled=True)),
                axis=1,
            ),
        )
        partials.append(jnp.sum(running))
        totals.append(global_sum(partials[-1]))
    potentials = jnp.stack(totals)
    rows_total = points.shape[0] * lax.axis_size("dp") * lax.axis_size("shard")
    weights = running * (rows_total / potentials[-1])
    return (running, weights, potentials)


def body(points, first_center, counts, cand_index):
    if one_holder(points, counts, cand_index):
        return fused(points, first_center, counts, cand_index)
    return separate(points, first_center, counts, cand_index)


def solution(mesh):
    placed = (P(("dp", "shard"), None), P(), P(None, "dp", "shard"), P(None, "dp", "shard", None))
    return jax.shard_map(
        body,
        mesh=mesh,
        in_specs=placed,
        out_specs=(P(("dp", "shard")), P(("dp", "shard")), P()),
        check_vma=False,
    )
```

```python
import functools

import jax
import jax.numpy as jnp
from jax import lax
from jax.experimental import pallas as pl
from jax.experimental.pallas import tpu as pltpu
from jax.sharding import PartitionSpec as P

CANDS_ALL = 512
QUAD = 4
TILE_ROWS = 16
LANES = 128
VMEM_GRANT = 62 * 1024 * 1024
MESH = pl.DeviceIdType.MESH
CONTRACT_LAST = (((1,), (1,)), ((), ()))
CONTRACT_FIRST = (((0,), (0,)), ((), ()))


def round_kernel(
    groups,
    width,
    pts_hbm,
    fc_hbm,
    cnt_hbm,
    idx_hbm,
    run_hbm,
    wgt_hbm,
    pot_hbm,
    run_ref,
    wgt_ref,
    pot_ref,
    fc_ref,
    cnt_ref,
    idx_ref,
    pts,
    packed,
    parts,
    cand,
    least_out,
    least_in,
    all_sums,
    local_sems,
    out_sems,
    part_send,
    part_recv,
    plane_send,
    plane_recv,
    class_send,
    class_recv,
    core_send,
    core_recv,
    z_send,
    z_recv,
    fwd_send,
    fwd_recv,
    least_send,
    least_recv,
    sum_send,
    sum_recv,
):
    rounds, total = idx_ref.shape[0], idx_ref.shape[3]
    rows, depth = pts_hbm.shape
    each = total // width
    classes = groups // QUAD
    chunks = z_send.shape[0]
    chunk = rows // chunks

    dp, me = lax.axis_index("dp"), lax.axis_index("shard")
    pieces = [(0, 1), (1, rounds)] if rounds > 1 else [(0, rounds)]
    cls, mine = dp // QUAD, dp % QUAD
    zside, core = mine // 2, mine % 2
    partner = zside * 2 + (1 - core)
    across = (1 - zside) * 2 + core
    diagonal = (1 - zside) * 2 + (1 - core)

    xpeer, ypeer = me + 1 - 2 * (me % 2), (me + 2) % width
    corner = (xpeer + 2) % width
    via = xpeer * (1 - core) + ypeer * core
    onto = ypeer * (1 - core) + xpeer * core

    def copy(src, dst, send, recv, to):
        made = pltpu.make_async_remote_copy(
            src_ref=src, dst_ref=dst, send_sem=send, recv_sem=recv, device_id=to, device_id_type=MESH
        )
        made.start()
        sent.append(made)

    def arrived(dst, send, recv):
        pltpu.make_async_remote_copy(
            src_ref=dst,
            dst_ref=dst,
            send_sem=send,
            recv_sem=recv,
            device_id=(dp, lax.rem(me + 1, width)),
            device_id_type=MESH,
        ).wait_recv()

    sent = []
    in_quad = lambda k: (cls * QUAD + k, me)
    in_plane = lambda off: (dp, lax.rem(me + off, width))
    anyone = lambda a, b: (lax.rem(dp + a * QUAD, groups), lax.rem(me + b, width))
    in_class = lambda off: anyone(off, 0)

    loads = [
        pltpu.make_async_copy(src, dst, local_sems.at[j])
        for j, (src, dst) in enumerate(
            (
                (idx_hbm, idx_ref),
                (cnt_hbm, cnt_ref),
                (pts_hbm, pts.at[mine]),
                (fc_hbm, fc_ref),
            )
        )
    ]
    for load in loads:
        load.start()
    barrier = pltpu.get_barrier_semaphore()
    for off in range(1, width):
        pl.semaphore_signal(barrier, inc=1, device_id=in_plane(off), device_id_type=MESH)
    for k in (partner, across, diagonal):
        pl.semaphore_signal(barrier, inc=1, device_id=in_quad(k), device_id_type=MESH)
    for a in range(1, classes):
        for b in range(width):
            pl.semaphore_signal(barrier, inc=1, device_id=anyone(a, b), device_id_type=MESH)

    def cross(j):
        span = pl.ds(j * chunk, chunk)
        copy(pts_hbm.at[span], pts.at[mine, span], z_send.at[j], z_recv.at[j], in_quad(across))

    pl.semaphore_wait(barrier, classes * width - 1 + QUAD - 1)
    for j in range(chunks - 1):
        cross(j)
    for load in loads[:3]:
        load.wait()
    spot = lax.broadcasted_iota(jnp.int32, (rows, total), 0)
    slot = lax.broadcasted_iota(jnp.int32, (rows, total), 1)
    for p, (t0, t1) in enumerate(pieces):
        hits = [(spot == idx_ref[t, 0]) & (slot < cnt_ref[t]) for t in range(t0, t1)]
        chosen = lax.dot_general(
            jnp.concatenate([jnp.where(hit, 1.0, 0.0) for hit in hits], axis=1).astype(pts.dtype),
            pts[mine],
            CONTRACT_FIRST,
            preferred_element_type=jnp.float32,
        ).astype(packed.dtype)
        for t in range(t0, t1):
            at = (t - t0) * total
            packed[:, t] = chosen[at : at + total].reshape(width, each, depth)
        for off in range(1, width):
            copy(
                packed.at[lax.rem(me + off, width), t0:t1],
                parts.at[me, t0:t1],
                part_send.at[p, off - 1],
                part_recv.at[p, off - 1],
                in_plane(off),
            )
    copy(pts_hbm, pts.at[mine], core_send, core_recv, in_quad(partner))

    squares = jnp.square(pts[mine].astype(jnp.float32))
    lanes = squares[:, :LANES]
    for j in range(1, depth // LANES):
        lanes = lanes + squares[:, j * LANES : (j + 1) * LANES]
    rows_norm = jnp.sum(lanes.T, axis=0, keepdims=True)
    loads[3].wait()
    first = fc_ref[...].reshape(1, depth)
    first_norm = jnp.sum(jnp.square(first.astype(jnp.float32)), axis=1, keepdims=True)
    first_prod = lax.dot_general(
        jnp.broadcast_to(first, (TILE_ROWS, depth)),
        pts[mine],
        CONTRACT_LAST,
        preferred_element_type=jnp.float32,
    )[:1]
    running = jnp.maximum(rows_norm + first_norm - 2.0 * first_prod, 0.0)

    def spread(c, at, p):
        t0, t1 = pieces[p]
        for off in range(1, width):
            copy(
                cand.at[c, me, t0:t1],
                cand.at[c, me, t0:t1],
                plane_send.at[at, p, off - 1],
                plane_recv.at[at, p, off - 1],
                in_plane(off),
            )

    for p, (t0, t1) in enumerate(pieces):
        held = packed[me, t0:t1].astype(jnp.float32)
        for off in range(1, width):
            source = lax.rem(me - off + width, width)
            arrived(parts.at[source, t0:t1], part_send.at[p, off - 1], part_recv.at[p, off - 1])
            held = held + parts[source, t0:t1].astype(jnp.float32)
        cand[cls, me, t0:t1] = held.astype(cand.dtype)
        for off in range(1, classes):
            copy(
                cand.at[cls, me, t0:t1],
                cand.at[cls, me, t0:t1],
                class_send.at[p, off - 1],
                class_recv.at[p, off - 1],
                in_class(off),
            )
        for at, peer in enumerate((xpeer, ypeer)):
            copy(
                cand.at[cls, me, t0:t1],
                cand.at[cls, me, t0:t1],
                plane_send.at[0, p, at],
                plane_recv.at[0, p, at],
                (dp, peer),
            )
    cross(chunks - 1)
    for p, (t0, t1) in enumerate(pieces):
        for at, peer in enumerate((xpeer, ypeer)):
            arrived(cand.at[cls, peer, t0:t1], plane_send.at[0, p, at], plane_recv.at[0, p, at])
        copy(
            cand.at[cls, via, t0:t1],
            cand.at[cls, via, t0:t1],
            plane_send.at[0, p, 2],
            plane_recv.at[0, p, 2],
            (dp, onto),
        )
        for off in range(1, classes):
            source = lax.rem(cls - off + classes, classes)
            arrived(
                cand.at[source, me, t0:t1], class_send.at[p, off - 1], class_recv.at[p, off - 1]
            )
            spread(source, off, p)

    def forward(j):
        span = pl.ds(j * chunk, chunk)
        arrived(pts.at[across, span], z_send.at[j], z_recv.at[j])
        copy(
            pts.at[across, span], pts.at[across, span], fwd_send.at[j], fwd_recv.at[j], in_quad(partner)
        )

    for j in range(chunks - 1):
        forward(j)

    def least(c, t0, t1, names):
        centers = cand[c, :, t0:t1].reshape(width * (t1 - t0) * each, depth)
        norms = jnp.sum(jnp.square(centers.astype(jnp.float32)), axis=1, keepdims=True)
        for name in names:
            if callable(name):
                name()
                continue
            prod = lax.dot_general(
                centers, pts[places[name]], CONTRACT_LAST, preferred_element_type=jnp.float32
            )
            dist = (norms - 2.0 * prod).reshape(width, t1 - t0, each, rows)
            this = jnp.min(jnp.min(dist, axis=0), axis=1)
            for t in range(t0, t1):
                row = this[t - t0 : t - t0 + 1]
                old = found.get((name, t))
                found[name, t] = row if old is None else jnp.minimum(old, row)

    def gathered(at, p):
        t0, t1 = pieces[p]
        c = lax.rem(cls - at + classes, classes)
        if at == 0:
            arrived(cand.at[cls, corner, t0:t1], plane_send.at[0, p, 2], plane_recv.at[0, p, 2])
            return c
        for off in range(1, width):
            source = lax.rem(me - off + width, width)
            arrived(
                cand.at[c, source, t0:t1],
                plane_send.at[at, p, off - 1],
                plane_recv.at[at, p, off - 1],
            )
        return c

    def across_ready():
        forward(chunks - 1)

    def diagonal_ready():
        for j in range(chunks):
            span = pl.ds(j * chunk, chunk)
            arrived(pts.at[diagonal, span], fwd_send.at[j], fwd_recv.at[j])

    places = (mine, partner, across, diagonal)
    found = {}
    tall = least_out.shape[0]
    least_out[QUAD * rounds :] = jnp.concatenate(
        [rows_norm, running]
        + [jnp.zeros_like(running)] * (tall - QUAD * rounds - 2),
        axis=0,
    )
    for p in range(len(pieces)):
        c = gathered(0, p)
    arrived(pts.at[partner], core_send, core_recv)
    least(c, 0, rounds, (0, 1, across_ready, 2, diagonal_ready, 3))
    for at in range(1, classes):
        for p, (t0, t1) in enumerate(pieces):
            c = gathered(at, p)
            least(c, t0, t1, range(QUAD))
    least_out[: QUAD * rounds] = jnp.concatenate(
        [found[name, t] for name in range(QUAD) for t in range(rounds)], axis=0
    )

    for at, k in enumerate((partner, across, diagonal)):
        copy(least_out, least_in.at[at], least_send.at[at], least_recv.at[at], in_quad(k))
    told = [least_out[...]]
    for at in range(QUAD - 1):
        arrived(least_in.at[at], least_send.at[at], least_recv.at[at])
        told.append(least_in[at])

    def fold(row):
        out = row[:, :LANES]
        for j in range(1, rows // LANES):
            out = out + row[:, j * LANES : (j + 1) * LANES]
        return out

    def block_rows(block):
        near = told[block][0:rounds]
        for at in range(QUAD):
            if at == block:
                continue
            from_row = (at ^ block) * rounds
            near = jnp.minimum(near, told[at][from_row : from_row + rounds])
        norm = told[block][QUAD * rounds : QUAD * rounds + 1]
        steps = [told[block][QUAD * rounds + 1 : QUAD * rounds + 2]]
        for t in range(rounds):
            steps.append(jnp.minimum(steps[-1], jnp.maximum(norm + near[t : t + 1], 0.0)))
        return steps

    blocks = [block_rows(block) for block in range(QUAD)]
    running = blocks[0][-1]
    run_ref[...] = running
    leaving = [
        pltpu.make_async_copy(src, dst, out_sems.at[j])
        for j, (src, dst) in enumerate(((run_ref, run_hbm), (wgt_ref, wgt_hbm), (pot_ref, pot_hbm)))
    ]
    leaving[0].start()
    partials = [
        (fold(blocks[0][t]) + fold(blocks[1][t])) + (fold(blocks[2][t]) + fold(blocks[3][t]))
        for t in range(rounds + 1)
    ]
    partials += [jnp.zeros_like(partials[0])] * (all_sums.shape[2] - len(partials))
    all_sums[cls, me] = jnp.concatenate(partials, axis=0)
    others = [(a, b) for a in range(classes) for b in range(width) if a or b]
    for a, b in others:
        copy(
            all_sums.at[cls, me],
            all_sums.at[cls, me],
            sum_send.at[a, b],
            sum_recv.at[a, b],
            anyone(a, b),
        )
    for a, b in others:
        source = (lax.rem(cls - a + classes, classes), lax.rem(me - b + width, width))
        arrived(all_sums.at[source], sum_send.at[a, b], sum_recv.at[a, b])
    sums = jnp.sum(
        jnp.sum(all_sums[...].reshape(classes * width, all_sums.shape[2], LANES), axis=0),
        axis=1,
        keepdims=True,
    )
    rows_all = rows * groups * width
    wgt_ref[...] = running * (rows_all / sums[rounds : rounds + 1])
    for t in range(rounds + 1):
        pot_ref[t] = sums[t, 0]
    for made in leaving[1:]:
        made.start()
    for made in sent:
        made.wait_send()
    for made in leaving:
        made.wait()


def hand_on(*refs):
    *arrays, sems = refs
    count = len(arrays) // 2
    copies = [
        pltpu.make_async_copy(arrays[j], arrays[count + j], sems.at[j]) for j in range(count)
    ]
    for each in copies:
        each.start()
    for each in copies:
        each.wait()


def fused(points, first_center, counts, cand_index):
    rows, depth = points.shape
    rounds, total = counts.shape[0], cand_index.shape[3]
    groups, width = lax.axis_size("dp"), lax.axis_size("shard")
    each, classes = total // width, groups // QUAD
    chunks, tall = 4, (QUAD * rounds + 2 + 7) // 8 * 8
    f32, held = jnp.float32, points.dtype
    dma = pltpu.SemaphoreType.DMA
    hbm = pl.BlockSpec(memory_space=pltpu.HBM)
    running, weights, potentials = pl.pallas_call(
        functools.partial(round_kernel, groups, width),
        out_shape=(
            jax.ShapeDtypeStruct((1, rows), f32),
            jax.ShapeDtypeStruct((1, rows), f32),
            jax.ShapeDtypeStruct((rounds + 1,), f32),
        ),
        in_specs=[hbm] * 4,
        out_specs=[hbm] * 3,
        scratch_shapes=[
            pltpu.VMEM((1, rows), f32),
            pltpu.VMEM((1, rows), f32),
            pltpu.SMEM((rounds + 1,), f32),
            pltpu.VMEM((depth,), held),
            pltpu.SMEM((rounds,), counts.dtype),
            pltpu.VMEM(cand_index.shape, cand_index.dtype),
            pltpu.VMEM((QUAD, rows, depth), held),
            pltpu.VMEM((width, rounds, each, depth), held),
            pltpu.VMEM((width, rounds, each, depth), held),
            pltpu.VMEM((classes, width, rounds, each, depth), held),
            pltpu.VMEM((tall, rows), f32),
            pltpu.VMEM((QUAD - 1, tall, rows), f32),
            pltpu.VMEM((classes, width, 8, LANES), f32),
            dma((4,)),
            dma((3,)),
            dma((2, width - 1)),
            dma((2, width - 1)),
            dma((classes, 2, width - 1)),
            dma((classes, 2, width - 1)),
            dma((2, max(classes - 1, 1))),
            dma((2, max(classes - 1, 1))),
            dma,
            dma,
            dma((chunks,)),
            dma((chunks,)),
            dma((chunks,)),
            dma((chunks,)),
            dma((QUAD - 1,)),
            dma((QUAD - 1,)),
            dma((classes, width)),
            dma((classes, width)),
        ],
        compiler_params=pltpu.CompilerParams(
            collective_id=0, has_side_effects=True, vmem_limit_bytes=VMEM_GRANT
        ),
    )(
        points,
        first_center,
        counts.reshape(rounds),
        cand_index,
    )
    made = (running.reshape(rows), weights.reshape(rows), potentials)
    return pl.pallas_call(
        hand_on,
        out_shape=[jax.ShapeDtypeStruct(part.shape, part.dtype) for part in made],
        in_specs=[hbm] * len(made),
        out_specs=[hbm] * len(made),
        scratch_shapes=[dma((len(made),))],
        compiler_params=pltpu.CompilerParams(vmem_limit_bytes=VMEM_GRANT),
    )(*made)


def one_holder(points, counts, cand_index):
    rows, depth = points.shape
    groups, width = lax.axis_size("dp"), lax.axis_size("shard")
    total = CANDS_ALL // groups
    return (
        cand_index.shape[3] == total
        and groups % QUAD == 0
        and width == 4
        and total % (width * TILE_ROWS) == 0
        and rows % (2 * LANES) == 0
        and depth % LANES == 0
        and counts.shape[0] < 8
    )


def pair_dist(rows, rows_norm, cands):
    prod = jnp.dot(rows, cands.T, preferred_element_type=jnp.float32)
    cand_norm = jnp.sum(jnp.square(cands.astype(jnp.float32)), axis=1)
    return jnp.maximum(rows_norm[:, None] + cand_norm[None, :] - 2.0 * prod, 0.0)


def pack_group(group_rows, member_counts, total, stride):
    ends = jnp.cumsum(member_counts)
    begins = ends - member_counts
    slot = jnp.arange(total, dtype=jnp.int32)
    source = jnp.sum((slot[:, None] >= ends[None, :]).astype(jnp.int32), axis=1)
    offset = slot - jnp.take(begins, source)
    return jnp.take(group_rows, source * stride + offset, axis=0)


def separate(points, first_center, counts, cand_index):
    rows_norm = jnp.sum(jnp.square(points.astype(jnp.float32)), axis=1)
    running = jnp.min(pair_dist(points, rows_norm, first_center[None, :]), axis=1)
    rounds = counts.shape[0]
    cap = cand_index.shape[3]
    every_count = lax.all_gather(counts.reshape(rounds, 1), ("dp", "shard"), axis=1, tiled=True)

    def global_sum(value):
        return lax.psum(value, ("dp", "shard"))

    partials = [jnp.sum(running)]
    totals = [global_sum(partials[0])]
    for step in range(rounds):
        local_rows = jnp.take(points, cand_index[step, 0, 0], axis=0)
        group_rows = lax.all_gather(local_rows, "shard", axis=0, tiled=True)
        width = lax.axis_size("shard")
        member_counts = lax.dynamic_slice_in_dim(
            every_count[step], lax.axis_index("dp") * width, width
        )
        total = CANDS_ALL // lax.axis_size("dp")
        packed = pack_group(group_rows, member_counts, total, cap)
        running = jnp.minimum(
            running,
            jnp.min(
                pair_dist(points, rows_norm, lax.all_gather(packed, "dp", axis=0, tiled=True)),
                axis=1,
            ),
        )
        partials.append(jnp.sum(running))
        totals.append(global_sum(partials[-1]))
    potentials = jnp.stack(totals)
    rows_total = points.shape[0] * lax.axis_size("dp") * lax.axis_size("shard")
    weights = running * (rows_total / potentials[-1])
    return (running, weights, potentials)


def body(points, first_center, counts, cand_index):
    if one_holder(points, counts, cand_index):
        return fused(points, first_center, counts, cand_index)
    return separate(points, first_center, counts, cand_index)


def solution(mesh):
    placed = (P(("dp", "shard"), None), P(), P(None, "dp", "shard"), P(None, "dp", "shard", None))
    return jax.shard_map(
        body,
        mesh=mesh,
        in_specs=placed,
        out_specs=(P(("dp", "shard")), P(("dp", "shard")), P()),
        check_vma=False,
    )
```

```python
import functools

import jax
import jax.numpy as jnp
from jax import lax
from jax.experimental import pallas as pl
from jax.experimental.pallas import tpu as pltpu
from jax.sharding import PartitionSpec as P

CANDS_ALL = 512
QUAD = 4
TILE_ROWS = 16
LANES = 128
VMEM_GRANT = 62 * 1024 * 1024
MESH = pl.DeviceIdType.MESH
CONTRACT_LAST = (((1,), (1,)), ((), ()))
CONTRACT_FIRST = (((0,), (0,)), ((), ()))


def round_kernel(
    groups,
    width,
    pts_hbm,
    fc_hbm,
    cnt_hbm,
    idx_hbm,
    run_hbm,
    wgt_hbm,
    pot_hbm,
    run_ref,
    wgt_ref,
    pot_ref,
    fc_ref,
    cnt_ref,
    idx_ref,
    pts,
    packed,
    parts,
    cand,
    least_out,
    least_in,
    all_sums,
    local_sems,
    out_sems,
    part_send,
    part_recv,
    plane_send,
    plane_recv,
    class_send,
    class_recv,
    core_send,
    core_recv,
    z_send,
    z_recv,
    fwd_send,
    fwd_recv,
    least_send,
    least_recv,
    sum_send,
    sum_recv,
):
    rounds, total = idx_ref.shape[0], idx_ref.shape[3]
    rows, depth = pts_hbm.shape
    each = total // width
    classes = groups // QUAD
    chunks = z_send.shape[0]
    chunk = rows // chunks

    dp, me = lax.axis_index("dp"), lax.axis_index("shard")
    pieces = [(0, rounds - 1), (rounds - 1, rounds)] if rounds > 1 else [(0, rounds)]
    cls, mine = dp // QUAD, dp % QUAD
    zside, core = mine // 2, mine % 2
    partner = zside * 2 + (1 - core)
    across = (1 - zside) * 2 + core
    diagonal = (1 - zside) * 2 + (1 - core)

    def copy(src, dst, send, recv, to):
        made = pltpu.make_async_remote_copy(
            src_ref=src, dst_ref=dst, send_sem=send, recv_sem=recv, device_id=to, device_id_type=MESH
        )
        made.start()
        sent.append(made)

    def arrived(dst, send, recv):
        pltpu.make_async_remote_copy(
            src_ref=dst,
            dst_ref=dst,
            send_sem=send,
            recv_sem=recv,
            device_id=(dp, lax.rem(me + 1, width)),
            device_id_type=MESH,
        ).wait_recv()

    sent = []
    in_quad = lambda k: (cls * QUAD + k, me)
    in_plane = lambda off: (dp, lax.rem(me + off, width))
    anyone = lambda a, b: (lax.rem(dp + a * QUAD, groups), lax.rem(me + b, width))
    in_class = lambda off: anyone(off, 0)

    loads = [
        pltpu.make_async_copy(src, dst, local_sems.at[j])
        for j, (src, dst) in enumerate(
            (
                (idx_hbm, idx_ref),
                (cnt_hbm, cnt_ref),
                (pts_hbm, pts.at[mine]),
                (fc_hbm, fc_ref),
            )
        )
    ]
    for load in loads:
        load.start()
    barrier = pltpu.get_barrier_semaphore()
    for off in range(1, width):
        pl.semaphore_signal(barrier, inc=1, device_id=in_plane(off), device_id_type=MESH)
    for k in (partner, across, diagonal):
        pl.semaphore_signal(barrier, inc=1, device_id=in_quad(k), device_id_type=MESH)
    for a in range(1, classes):
        for b in range(width):
            pl.semaphore_signal(barrier, inc=1, device_id=anyone(a, b), device_id_type=MESH)

    def cross(j):
        span = pl.ds(j * chunk, chunk)
        copy(pts_hbm.at[span], pts.at[mine, span], z_send.at[j], z_recv.at[j], in_quad(across))

    pl.semaphore_wait(barrier, classes * width - 1 + QUAD - 1)
    for j in range(chunks - 1):
        cross(j)
    for load in loads[:3]:
        load.wait()
    spot = lax.broadcasted_iota(jnp.int32, (rows, total), 0)
    slot = lax.broadcasted_iota(jnp.int32, (rows, total), 1)
    for p, (t0, t1) in enumerate(pieces):
        hits = [(spot == idx_ref[t, 0]) & (slot < cnt_ref[t]) for t in range(t0, t1)]
        chosen = lax.dot_general(
            jnp.concatenate([jnp.where(hit, 1.0, 0.0) for hit in hits], axis=1).astype(pts.dtype),
            pts[mine],
            CONTRACT_FIRST,
            preferred_element_type=jnp.float32,
        ).astype(packed.dtype)
        for t in range(t0, t1):
            at = (t - t0) * total
            packed[:, t] = chosen[at : at + total].reshape(width, each, depth)
        for off in range(1, width):
            copy(
                packed.at[lax.rem(me + off, width), t0:t1],
                parts.at[me, t0:t1],
                part_send.at[p, off - 1],
                part_recv.at[p, off - 1],
                in_plane(off),
            )
    copy(pts_hbm, pts.at[mine], core_send, core_recv, in_quad(partner))

    squares = jnp.square(pts[mine].astype(jnp.float32))
    lanes = squares[:, :LANES]
    for j in range(1, depth // LANES):
        lanes = lanes + squares[:, j * LANES : (j + 1) * LANES]
    rows_norm = jnp.sum(lanes.T, axis=0, keepdims=True)
    loads[3].wait()
    first = fc_ref[...].reshape(1, depth)
    first_norm = jnp.sum(jnp.square(first.astype(jnp.float32)), axis=1, keepdims=True)
    first_prod = lax.dot_general(
        jnp.broadcast_to(first, (TILE_ROWS, depth)),
        pts[mine],
        CONTRACT_LAST,
        preferred_element_type=jnp.float32,
    )[:1]
    running = jnp.maximum(rows_norm + first_norm - 2.0 * first_prod, 0.0)

    def spread(c, at, p):
        t0, t1 = pieces[p]
        for off in range(1, width):
            copy(
                cand.at[c, me, t0:t1],
                cand.at[c, me, t0:t1],
                plane_send.at[at, p, off - 1],
                plane_recv.at[at, p, off - 1],
                in_plane(off),
            )

    for p, (t0, t1) in enumerate(pieces):
        held = packed[me, t0:t1].astype(jnp.float32)
        for off in range(1, width):
            source = lax.rem(me - off + width, width)
            arrived(parts.at[source, t0:t1], part_send.at[p, off - 1], part_recv.at[p, off - 1])
            held = held + parts[source, t0:t1].astype(jnp.float32)
        cand[cls, me, t0:t1] = held.astype(cand.dtype)
        for off in range(1, classes):
            copy(
                cand.at[cls, me, t0:t1],
                cand.at[cls, me, t0:t1],
                class_send.at[p, off - 1],
                class_recv.at[p, off - 1],
                in_class(off),
            )
        spread(cls, 0, p)
    cross(chunks - 1)
    for p, (t0, t1) in enumerate(pieces):
        for off in range(1, classes):
            source = lax.rem(cls - off + classes, classes)
            arrived(
                cand.at[source, me, t0:t1], class_send.at[p, off - 1], class_recv.at[p, off - 1]
            )
            spread(source, off, p)

    def forward(j):
        span = pl.ds(j * chunk, chunk)
        arrived(pts.at[across, span], z_send.at[j], z_recv.at[j])
        copy(
            pts.at[across, span], pts.at[across, span], fwd_send.at[j], fwd_recv.at[j], in_quad(partner)
        )

    for j in range(chunks - 1):
        forward(j)

    def least(c, t0, t1, names):
        centers = cand[c, :, t0:t1].reshape(width * (t1 - t0) * each, depth)
        norms = jnp.sum(jnp.square(centers.astype(jnp.float32)), axis=1, keepdims=True)
        for name in names:
            if callable(name):
                name()
                continue
            prod = lax.dot_general(
                centers, pts[places[name]], CONTRACT_LAST, preferred_element_type=jnp.float32
            )
            dist = (norms - 2.0 * prod).reshape(width, t1 - t0, each, rows)
            this = jnp.min(jnp.min(dist, axis=0), axis=1)
            for t in range(t0, t1):
                row = this[t - t0 : t - t0 + 1]
                old = found.get((name, t))
                found[name, t] = row if old is None else jnp.minimum(old, row)

    def gathered(at, p):
        t0, t1 = pieces[p]
        c = lax.rem(cls - at + classes, classes)
        for off in range(1, width):
            source = lax.rem(me - off + width, width)
            arrived(
                cand.at[c, source, t0:t1],
                plane_send.at[at, p, off - 1],
                plane_recv.at[at, p, off - 1],
            )
        return c

    def across_ready():
        forward(chunks - 1)

    def diagonal_ready():
        for j in range(chunks):
            span = pl.ds(j * chunk, chunk)
            arrived(pts.at[diagonal, span], fwd_send.at[j], fwd_recv.at[j])

    places = (mine, partner, across, diagonal)
    found = {}
    tall = least_out.shape[0]
    least_out[QUAD * rounds :] = jnp.concatenate(
        [rows_norm, running]
        + [jnp.zeros_like(running)] * (tall - QUAD * rounds - 2),
        axis=0,
    )
    for p in range(len(pieces)):
        c = gathered(0, p)
    arrived(pts.at[partner], core_send, core_recv)
    least(c, 0, rounds, (0, 1, across_ready, 2, diagonal_ready, 3))
    for at in range(1, classes):
        for p, (t0, t1) in enumerate(pieces):
            c = gathered(at, p)
            least(c, t0, t1, range(QUAD))
    least_out[: QUAD * rounds] = jnp.concatenate(
        [found[name, t] for name in range(QUAD) for t in range(rounds)], axis=0
    )

    for at, k in enumerate((partner, across, diagonal)):
        copy(least_out, least_in.at[at], least_send.at[at], least_recv.at[at], in_quad(k))
    told = [least_out[...]]
    for at in range(QUAD - 1):
        arrived(least_in.at[at], least_send.at[at], least_recv.at[at])
        told.append(least_in[at])

    def fold(row):
        out = row[:, :LANES]
        for j in range(1, rows // LANES):
            out = out + row[:, j * LANES : (j + 1) * LANES]
        return out

    def block_rows(block):
        near = told[block][0:rounds]
        for at in range(QUAD):
            if at == block:
                continue
            from_row = (at ^ block) * rounds
            near = jnp.minimum(near, told[at][from_row : from_row + rounds])
        norm = told[block][QUAD * rounds : QUAD * rounds + 1]
        steps = [told[block][QUAD * rounds + 1 : QUAD * rounds + 2]]
        for t in range(rounds):
            steps.append(jnp.minimum(steps[-1], jnp.maximum(norm + near[t : t + 1], 0.0)))
        return steps

    blocks = [block_rows(block) for block in range(QUAD)]
    running = blocks[0][-1]
    run_ref[...] = running
    leaving = [
        pltpu.make_async_copy(src, dst, out_sems.at[j])
        for j, (src, dst) in enumerate(((run_ref, run_hbm), (wgt_ref, wgt_hbm), (pot_ref, pot_hbm)))
    ]
    leaving[0].start()
    partials = [
        (fold(blocks[0][t]) + fold(blocks[1][t])) + (fold(blocks[2][t]) + fold(blocks[3][t]))
        for t in range(rounds + 1)
    ]
    partials += [jnp.zeros_like(partials[0])] * (all_sums.shape[2] - len(partials))
    all_sums[cls, me] = jnp.concatenate(partials, axis=0)
    others = [(a, b) for a in range(classes) for b in range(width) if a or b]
    for a, b in others:
        copy(
            all_sums.at[cls, me],
            all_sums.at[cls, me],
            sum_send.at[a, b],
            sum_recv.at[a, b],
            anyone(a, b),
        )
    for a, b in others:
        source = (lax.rem(cls - a + classes, classes), lax.rem(me - b + width, width))
        arrived(all_sums.at[source], sum_send.at[a, b], sum_recv.at[a, b])
    sums = jnp.sum(
        jnp.sum(all_sums[...].reshape(classes * width, all_sums.shape[2], LANES), axis=0),
        axis=1,
        keepdims=True,
    )
    rows_all = rows * groups * width
    wgt_ref[...] = running * (rows_all / sums[rounds : rounds + 1])
    for t in range(rounds + 1):
        pot_ref[t] = sums[t, 0]
    for made in leaving[1:]:
        made.start()
    for made in sent:
        made.wait_send()
    for made in leaving:
        made.wait()


def hand_on(*refs):
    *arrays, sems = refs
    count = len(arrays) // 2
    copies = [
        pltpu.make_async_copy(arrays[j], arrays[count + j], sems.at[j]) for j in range(count)
    ]
    for each in copies:
        each.start()
    for each in copies:
        each.wait()


def fused(points, first_center, counts, cand_index):
    rows, depth = points.shape
    rounds, total = counts.shape[0], cand_index.shape[3]
    groups, width = lax.axis_size("dp"), lax.axis_size("shard")
    each, classes = total // width, groups // QUAD
    chunks, tall = 4, (QUAD * rounds + 2 + 7) // 8 * 8
    f32, held = jnp.float32, points.dtype
    dma = pltpu.SemaphoreType.DMA
    hbm = pl.BlockSpec(memory_space=pltpu.HBM)
    running, weights, potentials = pl.pallas_call(
        functools.partial(round_kernel, groups, width),
        out_shape=(
            jax.ShapeDtypeStruct((1, rows), f32),
            jax.ShapeDtypeStruct((1, rows), f32),
            jax.ShapeDtypeStruct((rounds + 1,), f32),
        ),
        in_specs=[hbm] * 4,
        out_specs=[hbm] * 3,
        scratch_shapes=[
            pltpu.VMEM((1, rows), f32),
            pltpu.VMEM((1, rows), f32),
            pltpu.SMEM((rounds + 1,), f32),
            pltpu.VMEM((depth,), held),
            pltpu.SMEM((rounds,), counts.dtype),
            pltpu.VMEM(cand_index.shape, cand_index.dtype),
            pltpu.VMEM((QUAD, rows, depth), held),
            pltpu.VMEM((width, rounds, each, depth), held),
            pltpu.VMEM((width, rounds, each, depth), held),
            pltpu.VMEM((classes, width, rounds, each, depth), held),
            pltpu.VMEM((tall, rows), f32),
            pltpu.VMEM((QUAD - 1, tall, rows), f32),
            pltpu.VMEM((classes, width, 8, LANES), f32),
            dma((4,)),
            dma((3,)),
            dma((2, width - 1)),
            dma((2, width - 1)),
            dma((classes, 2, width - 1)),
            dma((classes, 2, width - 1)),
            dma((2, max(classes - 1, 1))),
            dma((2, max(classes - 1, 1))),
            dma,
            dma,
            dma((chunks,)),
            dma((chunks,)),
            dma((chunks,)),
            dma((chunks,)),
            dma((QUAD - 1,)),
            dma((QUAD - 1,)),
            dma((classes, width)),
            dma((classes, width)),
        ],
        compiler_params=pltpu.CompilerParams(
            collective_id=0, has_side_effects=True, vmem_limit_bytes=VMEM_GRANT
        ),
    )(
        points,
        first_center,
        counts.reshape(rounds),
        cand_index,
    )
    made = (running.reshape(rows), weights.reshape(rows), potentials)
    return pl.pallas_call(
        hand_on,
        out_shape=[jax.ShapeDtypeStruct(part.shape, part.dtype) for part in made],
        in_specs=[hbm] * len(made),
        out_specs=[hbm] * len(made),
        scratch_shapes=[dma((len(made),))],
        compiler_params=pltpu.CompilerParams(vmem_limit_bytes=VMEM_GRANT),
    )(*made)


def one_holder(points, counts, cand_index):
    rows, depth = points.shape
    groups, width = lax.axis_size("dp"), lax.axis_size("shard")
    total = CANDS_ALL // groups
    return (
        cand_index.shape[3] == total
        and groups % QUAD == 0
        and width > 1
        and total % (width * TILE_ROWS) == 0
        and rows % (2 * LANES) == 0
        and depth % LANES == 0
        and counts.shape[0] < 8
    )


def pair_dist(rows, rows_norm, cands):
    prod = jnp.dot(rows, cands.T, preferred_element_type=jnp.float32)
    cand_norm = jnp.sum(jnp.square(cands.astype(jnp.float32)), axis=1)
    return jnp.maximum(rows_norm[:, None] + cand_norm[None, :] - 2.0 * prod, 0.0)


def pack_group(group_rows, member_counts, total, stride):
    ends = jnp.cumsum(member_counts)
    begins = ends - member_counts
    slot = jnp.arange(total, dtype=jnp.int32)
    source = jnp.sum((slot[:, None] >= ends[None, :]).astype(jnp.int32), axis=1)
    offset = slot - jnp.take(begins, source)
    return jnp.take(group_rows, source * stride + offset, axis=0)


def separate(points, first_center, counts, cand_index):
    rows_norm = jnp.sum(jnp.square(points.astype(jnp.float32)), axis=1)
    running = jnp.min(pair_dist(points, rows_norm, first_center[None, :]), axis=1)
    rounds = counts.shape[0]
    cap = cand_index.shape[3]
    every_count = lax.all_gather(counts.reshape(rounds, 1), ("dp", "shard"), axis=1, tiled=True)

    def global_sum(value):
        return lax.psum(value, ("dp", "shard"))

    partials = [jnp.sum(running)]
    totals = [global_sum(partials[0])]
    for step in range(rounds):
        local_rows = jnp.take(points, cand_index[step, 0, 0], axis=0)
        group_rows = lax.all_gather(local_rows, "shard", axis=0, tiled=True)
        width = lax.axis_size("shard")
        member_counts = lax.dynamic_slice_in_dim(
            every_count[step], lax.axis_index("dp") * width, width
        )
        total = CANDS_ALL // lax.axis_size("dp")
        packed = pack_group(group_rows, member_counts, total, cap)
        running = jnp.minimum(
            running,
            jnp.min(
                pair_dist(points, rows_norm, lax.all_gather(packed, "dp", axis=0, tiled=True)),
                axis=1,
            ),
        )
        partials.append(jnp.sum(running))
        totals.append(global_sum(partials[-1]))
    potentials = jnp.stack(totals)
    rows_total = points.shape[0] * lax.axis_size("dp") * lax.axis_size("shard")
    weights = running * (rows_total / potentials[-1])
    return (running, weights, potentials)


def body(points, first_center, counts, cand_index):
    if one_holder(points, counts, cand_index):
        return fused(points, first_center, counts, cand_index)
    return separate(points, first_center, counts, cand_index)


def solution(mesh):
    placed = (P(("dp", "shard"), None), P(), P(None, "dp", "shard"), P(None, "dp", "shard", None))
    return jax.shard_map(
        body,
        mesh=mesh,
        in_specs=placed,
        out_specs=(P(("dp", "shard")), P(("dp", "shard")), P()),
        check_vma=False,
    )
```
